512 devices in a mesh: expert: 64 (over y, x, z_hi, core), fsdp: 8 (over z_lo).
Axes of the slice: x: 4, y: 4, z: 16 (z_hi: 2, z_lo: 8; z = z_hi * 8 + z_lo), core: 2. Of those that a mesh axis runs over, the one named last changes fastest.
Arguments:
- tokens: bfloat16 [768, 4096], P('expert', 'fsdp'), may hold values from -6 to 6
- gain: float32 [4096], P('fsdp'), may hold values from 0.1 to 1.9
- w_sel: bfloat16 [4096, 64], P('fsdp'), may hold values from -0.09375 to 0.09375
- w_up: bfloat16 [64, 4096, 1024], P('expert', 'fsdp'), may hold values from -0.09375 to 0.09375
- w_down: bfloat16 [64, 1024, 4096], P('expert', None, 'fsdp'), may hold values from -0.1875 to 0.1875
- routes: int32 [2, 768, 8], P(None, 'expert'), may hold values from 0 to 63, all different within a row; in each aligned block of 12 rows (0 to 11, 12 to 23, ..., all dimensions but the last counted through in order) at most 3 rows name the same one
- cotangent: bfloat16 [768, 4096], P('expert', 'fsdp'), may hold values from -6 to 6
Outputs:
- mixed: bfloat16 [768, 4096], P('expert', 'fsdp')
- d_tokens: bfloat16 [768, 4096], P('expert', 'fsdp')
- d_w_up: bfloat16 [64, 4096, 1024], P('expert', 'fsdp')
- d_w_down: bfloat16 [64, 1024, 4096], P('expert', None, 'fsdp')
- d_w_sel: float32 [4096, 64], P('fsdp')
The draws below stay inside these ranges and needn't reach their ends.
Inputs may be any that keep to these rules, and one draw needn't show every extreme that they name: `routes`: each token names 8 different experts in each loop; in each loop each aligned block of 12 tokens names any one expert at most 3 times, and some block names some expert exactly 3 times.
All inputs are finite; a program needn't handle non-finite values.
Results may differ from the reference program's by a relative error of at most 0.019.
Values may be sent and summed in bfloat16 or wider, within the bound.
A program may use at most 64 MiB of HBM per device.

```python
import math
import jax
import jax.numpy as jnp
import numpy as np
from jax import lax

D = 4096
H = 1024
TOPK = 8
LOOPS = 2
TOK_GROUP = 12
EXPERTS = 64
CAP = 3
TOKENS = 768
N_EXPERT = 64


def block_scale(rng, extent, cuts, smallest, high):
    loudness, own = 1.0, jax.random.fold_in(rng, 6)
    for dim, shards_of in cuts:
        heights = jnp.exp(jax.random.uniform(jax.random.fold_in(own, dim), (shards_of,), jnp.float32, smallest / len(cuts), high / len(cuts)))
        loudness = loudness * jnp.repeat(heights, extent[dim] // shards_of).reshape([-1 if axis == dim else 1 for axis in range(len(extent))])
    return loudness


def deal_out(key, own, number, rows, number_of, top, most, slope):
    sequence = jax.random.permutation(key, number_of)
    packed, ordinary = portions_of(number_of, rows * top, most, slope, True), portions_of(number_of, rows * top, most, slope, False)
    places = jnp.arange(number_of)

    def named(lengths, offset_by):
        used = int((lengths > 0).sum())
        fixed = max(1, used // 4)
        passed = fixed + (places - fixed + offset_by * (used - fixed)) % max(1, number_of - fixed)
        return jnp.zeros((number_of,), jnp.int32).at[sequence[jnp.where(places < fixed, places, passed)]].set(jnp.asarray(lengths, jnp.int32))

    lengths = jnp.where(number % 4 == 0, named(packed, number // 4), named(ordinary, number - number // 4 - 1))
    mixed = jax.random.permutation(jax.random.fold_in(own, 3), number_of)
    source_of, receiver = mixed[0:number_of // 2 * 2:2], mixed[1:number_of // 2 * 2:2]
    margin = jnp.minimum(lengths[source_of] - 1, most - lengths[receiver]) // 2
    margin = jnp.where((source_of == sequence[0]) | (receiver == sequence[0]) | (lengths[receiver] == 0), 0, jnp.maximum(margin, 0))
    passed = jax.random.randint(jax.random.fold_in(own, 4), (number_of // 2,), 0, 1 << 20) % (margin + 1)
    lengths = lengths.at[source_of].add(-passed).at[receiver].add(passed)
    members = jnp.searchsorted(jnp.cumsum(lengths), jnp.arange(rows * top), side="right").astype(jnp.int32)
    listing = members.reshape(top, rows).T
    listing = listing[jax.random.permutation(jax.random.fold_in(own, 1), rows)]
    offset_by = jax.random.randint(jax.random.fold_in(own, 2), (rows, 1), 0, top)
    return jnp.take_along_axis(listing, (jnp.arange(top)[None, :] + offset_by) % top, axis=1)


def portions_of(amount, total, reach, skew, full):
    portions = [(1 << 20) // math.isqrt(standing ** skew) + 1 for standing in range(1, amount + 1)]
    largest = reach if full else min(reach, max(-(-total // amount), total * portions[0] // sum(portions)))
    least = 1 if total - largest >= amount - 1 else 0
    given, rest = [largest] + [least] * (amount - 1), total - largest - least * (amount - 1)
    while rest > 0:
        candidates = [i for i in range(1, amount) if given[i] < largest] or [i for i in range(1, amount) if given[i] < reach]
        mass, left = sum([portions[i] for i in candidates]), rest
        for i in candidates:
            addition = min(reach - given[i], max(1, left * portions[i] // mass), rest)
            given[i] = given[i] + addition
            rest = rest - addition
    return np.array(given)


def normal_values(stream_key, dims, spread, reach, shards=(), held_as=jnp.bfloat16):
    result = spread * jax.random.normal(stream_key, dims, jnp.float32)
    if shards:
        result = result * block_scale(stream_key, dims, shards, -0.22, 0.18)
    return jnp.clip(result, -reach, reach).astype(held_as)


def setup_inputs(seed: int = 0) -> dict:
    keys = jax.random.split(jax.random.key(seed), 8)
    tokens = normal_values(keys[0], (TOKENS, D), 1.0, 6.0, ((0, 64), (1, 8)))
    gain = jnp.clip(1.0 + 0.18 * jax.random.normal(keys[1], (D,), jnp.float32), 0.1, 1.9)
    w_sel = normal_values(keys[2], (D, EXPERTS), D ** -0.5, 0.09375, ((0, 8),))
    w_up = normal_values(keys[3], (EXPERTS, D, H), D ** -0.5, 0.09375, ((0, 64), (1, 8)))
    w_down = normal_values(keys[4], (EXPERTS, H, D), H ** -0.5, 0.1875, ((0, 64), (2, 8)))
    routes_keys = jax.random.split(jax.random.fold_in(keys[5], 1), LOOPS * TOKENS // TOK_GROUP)
    routes_turns = jax.random.permutation(jax.random.fold_in(keys[5], 3), LOOPS * TOKENS // TOK_GROUP)
    routes = jax.vmap(lambda own, number: deal_out(jax.random.fold_in(keys[5], 2), own, number, TOK_GROUP, EXPERTS, TOPK, CAP, 2))(routes_keys, routes_turns).reshape((LOOPS, TOKENS, TOPK))
    cotangent = normal_values(keys[6], (TOKENS, D), 1.0, 6.0, ((0, 64), (1, 8)))
    return {"tokens": tokens, "gain": gain, "w_sel": w_sel, "w_up": w_up, "w_down": w_down, "routes": routes, "cotangent": cotangent}


EPSILON = 1e-06
HIGHEST = lax.Precision.HIGHEST

def slot_rows(route_rows):
    blocks = route_rows.reshape(TOKENS // TOK_GROUP, TOK_GROUP * TOPK)
    marks = (blocks[:, :, None] == jnp.arange(EXPERTS, dtype=jnp.int32)[None, None, :]).astype(jnp.int32)
    earlier = jnp.cumsum(marks, axis=1) - marks
    slots = lax.optimization_barrier(jnp.sum(earlier * marks, axis=2)).astype(jnp.int32)
    owners = jnp.arange(TOKENS // TOK_GROUP, dtype=jnp.int32)[:, None] * CAP
    return (blocks.reshape(-1).astype(jnp.int32), (owners + slots).reshape(-1).astype(jnp.int32))

def silu_slope(pre):
    sig = jax.nn.sigmoid(pre)
    return sig * (1.0 + pre * (1.0 - sig))

def expert_forward(operands):
    arrived, up_proj, down_proj = operands
    total = jnp.einsum('rd,dh->hr', arrived.astype(jnp.float32), up_proj.astype(jnp.float32))
    hidden = (total * jax.nn.sigmoid(total)).astype(jnp.bfloat16)
    outputs = jnp.einsum('hr,hd->rd', hidden.astype(jnp.float32), down_proj.astype(jnp.float32))
    return (total, hidden, outputs.astype(jnp.bfloat16))

def expert_backward(operands):
    grad_rows, pre, up_proj, down_proj = operands
    total = jnp.einsum('rd,hd->hr', grad_rows.astype(jnp.float32), down_proj.astype(jnp.float32))
    hidden_grad = (total * silu_slope(pre)).astype(jnp.bfloat16)
    back_grad = jnp.einsum('hr,dh->rd', hidden_grad.astype(jnp.float32), up_proj.astype(jnp.float32))
    return (hidden_grad, back_grad.astype(jnp.bfloat16))

def weight_grads(operands):
    arrived, hidden, grad_rows, hidden_grad = operands
    up_grad = jnp.einsum('lrd,lhr->dh', arrived.astype(jnp.float32), hidden_grad.astype(jnp.float32))
    down_grad = jnp.einsum('lhr,lrd->hd', hidden.astype(jnp.float32), grad_rows.astype(jnp.float32))
    return (up_grad.astype(jnp.bfloat16), down_grad.astype(jnp.bfloat16))

def reference(tokens, gain, w_sel, w_up, w_down, routes, cotangent):
    row_count = N_EXPERT * CAP
    expert_ids = jnp.arange(EXPERTS, dtype=jnp.int32)
    current = tokens
    saved = []
    for loop_index in range(LOOPS):
        widened = current.astype(jnp.float32)
        inv_rms = lax.rsqrt(lax.optimization_barrier(jnp.sum(widened * widened, axis=1)) / D + EPSILON)
        normed = (widened * inv_rms[:, None] * gain[None, :]).astype(jnp.bfloat16)
        logits = jnp.dot(normed, w_sel, preferred_element_type=jnp.float32)
        chooser = (routes[loop_index][:, :, None] == expert_ids[None, None, :]).astype(jnp.float32)
        gates = jax.nn.sigmoid(lax.optimization_barrier(jnp.sum(chooser * logits[:, None, :], axis=2)))
        owners, rows = slot_rows(routes[loop_index])
        copies = jnp.repeat(normed, TOPK, axis=0)
        sent = jnp.zeros((EXPERTS, row_count, D), jnp.bfloat16).at[owners, rows].set(copies)
        pre, hidden, outputs = lax.map(expert_forward, (sent, w_up, w_down))
        back = outputs[owners, rows].reshape(TOKENS, TOPK, D)
        blend = lax.optimization_barrier(jnp.sum(gates[:, :, None] * back.astype(jnp.float32), axis=1))
        saved.append((current, inv_rms, normed, gates, chooser, owners, rows, sent, pre, hidden, back))
        current = (widened + blend).astype(jnp.bfloat16)
    mixed = current
    incoming = cotangent
    select_total = jnp.zeros((D, EXPERTS), jnp.float32)
    records = []
    for loop_index in reversed(range(LOOPS)):
        current, inv_rms, normed, gates, chooser, owners, rows, sent, pre, hidden, back = saved[loop_index]
        grad_wide = incoming.astype(jnp.float32)
        gate_grad = lax.optimization_barrier(jnp.sum(grad_wide[:, None, :] * back.astype(jnp.float32), axis=2))
        out_grad = (gates[:, :, None] * grad_wide[:, None, :]).astype(jnp.bfloat16).reshape(TOKENS * TOPK, D)
        d_sent = jnp.zeros((EXPERTS, row_count, D), jnp.bfloat16).at[owners, rows].set(out_grad)
        hidden_grad, back_grad = lax.map(expert_backward, (d_sent, pre, w_up, w_down))
        back_rows = back_grad[owners, rows].reshape(TOKENS, TOPK, D).astype(jnp.float32)
        logit_grad = gate_grad * gates * (1.0 - gates)
        logit_table = lax.optimization_barrier(jnp.sum(chooser * logit_grad[:, :, None], axis=1))
        normed_grad = lax.optimization_barrier(jnp.sum(back_rows, axis=1)) + jnp.dot(logit_table, w_sel.astype(jnp.float32).T, precision=HIGHEST)
        select_total = select_total + jnp.dot(normed.astype(jnp.float32).T, logit_table, precision=HIGHEST)
        widened = current.astype(jnp.float32)
        inner_sum = lax.optimization_barrier(jnp.sum(widened * gain[None, :] * normed_grad, axis=1))
        cube = inv_rms * inv_rms * inv_rms / D
        new_grad = grad_wide + inv_rms[:, None] * gain[None, :] * normed_grad - cube[:, None] * widened * inner_sum[:, None]
        incoming = new_grad.astype(jnp.bfloat16)
        records.append((sent, hidden, d_sent, hidden_grad))
    stacked = tuple((jnp.stack([entry[part] for entry in records], axis=1) for part in range(4)))
    up_grads, down_grads = lax.map(weight_grads, stacked)
    return (mixed, incoming, up_grads, down_grads, select_total)
```

```python
import functools
from types import SimpleNamespace

import jax
import jax.numpy as jnp
from jax import lax
from jax.experimental import pallas as pl
from jax.experimental.pallas import tpu as pltpu
from jax.sharding import PartitionSpec as P

EPSILON = 1e-06
HIGHEST = lax.Precision.HIGHEST
MESH = pl.DeviceIdType.MESH
BF, F32 = jnp.bfloat16, jnp.float32
PAD = 16
MARKS = 64


def iota(shape, dim):
    return lax.broadcasted_iota(jnp.int32, shape, dim)


def dot(a, b, ca, cb, precision=None):
    return lax.dot_general(
        a, b, (((ca,), (cb,)), ((), ())), precision=precision, preferred_element_type=F32
    )


def column(lanes):
    n = lanes.shape[1]
    return jnp.sum(jnp.where(iota((n, n), 0) == iota((n, n), 1), lanes, 0.0), axis=1, keepdims=True)


def two_rows(first, second):
    return jnp.where(iota(first.shape, 0) == 0, first, second)


def kernel(
    s,
    x_ref, cot_ref, gain_ref, sel_ref, up_ref, down_ref, routes_ref,
    mixed_ref, dtok_ref, dup_ref, ddown_ref, dsel_ref,
    ax, ac, a1, a2, asel,
    pbuf, rbuf, full, ebuf, gbuf,
    sb, sib, tb, rb, uf, ub, zb,
    pg, ps, pre_k, slope_k, hid_k, dh_k, rows, grads, up_acc, down_acc,
    fs_send, fs_recv, fx_send, fx_recv,
    ag_send, ag_recv, az_send, az_recv, as_send, as_recv,
    rs_send, rs_recv, rz_send, rz_recv, rb_send, rb_recv,
):
    Q, F, R, W, H, D = s.chips, s.fsdp, s.rows, s.width, s.hidden, s.model
    T = s.tokens
    HL = H // F
    half = Q * 2 * PAD
    e, z = lax.axis_index("expert"), lax.axis_index("fsdp")
    q, zh, c = e // 4, (e // 2) % 2, e % 2

    def place(q_, zh_, c_):
        return (q_ * 4 + zh_ * 2 + c_, z)

    far, twin = place(q, 1 - zh, c), place(q, zh, 1 - c)

    def chip(i):
        return lax.rem(q + i, Q)

    def line(i):
        return lax.rem(z + i, F)

    def copy(src, dst, send, recv, device):
        return pltpu.make_async_remote_copy(
            src_ref=src, dst_ref=dst, send_sem=send, recv_sem=recv, device_id=device, device_id_type=MESH
        )

    def each(count, fn):
        lax.fori_loop(1, count, lambda i, t: (fn(i), t)[1], 0)

    pending = []

    barrier = pltpu.get_barrier_semaphore()

    def greet(device):
        pl.semaphore_signal(barrier, inc=1, device_id=device, device_id_type=MESH)

    each(F, lambda i: greet((e, line(i))))
    each(Q, lambda i: greet(place(chip(i), zh, c)))
    greet(far)
    greet(twin)
    pl.semaphore_wait(barrier, F + Q)

    def ag_hop(k, a, wave, i):
        src = a.at[c, q, zh if wave == 0 else 1 - zh]
        return copy(src, src, ag_send.at[k, wave, i], ag_recv.at[k, wave, i], place(chip(i), zh, c))

    def ag_far(k, a):
        src = a.at[c, q, zh]
        return copy(src, src, az_send.at[k], az_recv.at[k], far)

    def ag_twin(k, a):
        return copy(a.at[c], a.at[c], as_send.at[k], as_recv.at[k], twin)

    def ag_start(k, a):
        ag_far(k, a).start()
        each(Q, lambda i: ag_hop(k, a, 0, i).start())

    def ag_forward(k, a):
        ag_far(k, a).wait_recv()
        each(Q, lambda i: ag_hop(k, a, 1, i).start())

    def ag_join(k, a):
        each(Q, lambda i: ag_hop(k, a, 0, i).wait_recv())
        each(Q, lambda i: ag_hop(k, a, 1, i).wait_recv())
        ag_twin(k, a).start()

    def ag_finish(k, a):
        ag_twin(k, a).wait_recv()

        def drain():
            ag_far(k, a).wait_send()
            each(Q, lambda i: ag_hop(k, a, 0, i).wait_send())
            each(Q, lambda i: ag_hop(k, a, 1, i).wait_send())
            ag_twin(k, a).wait_send()

        pending.append(drain)

    def fs_hop(k, i):
        return copy(pbuf.at[k, line(i)], rbuf.at[k, i], fs_send.at[k, i], fs_recv.at[k, i], (e, line(i)))

    def fs_ext(k, i):
        return copy(ebuf.at[k, 0], ebuf.at[k, i], fx_send.at[k, i], fx_recv.at[k, i], (e, line(i)))

    def fs_fill(k, value):
        for j in range(F):
            pbuf[k, j] = value[:, j * HL : (j + 1) * HL].astype(BF)

    def fs_start(k):
        each(F, lambda i: fs_hop(k, i).start())
        pending.append(lambda: each(F, lambda i: fs_hop(k, i).wait_send()))

    def fs_sum(k):
        total = pbuf[k, z].astype(F32)
        for i in range(1, F):
            fs_hop(k, i).wait_recv()
            total = total + rbuf[k, i].astype(F32)
        return total

    def ext_start(k, value):
        ebuf[k, 0] = value
        each(F, lambda i: fs_ext(k, i).start())
        pending.append(lambda: each(F, lambda i: fs_ext(k, i).wait_send()))

    def ext_sum(k):
        total = ebuf[k, 0]
        for i in range(1, F):
            fs_ext(k, i).wait_recv()
            total = total + ebuf[k, i]
        return total

    def fg_hop(k, i):
        return copy(full.at[k, z], full.at[k, z], fs_send.at[4 + k, i], fs_recv.at[4 + k, i], (e, line(i)))

    def fg_start(k, value):
        full[k, z] = value
        each(F, lambda i: fg_hop(k, i).start())
        pending.append(lambda: each(F, lambda i: fg_hop(k, i).wait_send()))

    def fg_wait(k):
        each(F, lambda i: fg_hop(k, i).wait_recv())

    def fg_value(k):
        return jnp.concatenate([full[k, j] for j in range(F)], axis=1)

    def rs_twin(k):
        return copy(sb.at[k], sib.at[k], rb_send.at[k], rb_recv.at[k], twin)

    def rs_hop(k, i):
        return copy(tb.at[k, chip(i)], rb.at[k, i], rs_send.at[k, i], rs_recv.at[k, i], place(chip(i), zh, c))

    def rs_far(k):
        return copy(ub.at[k], zb.at[k], rz_send.at[k], rz_recv.at[k], far)

    def rs_start(k, loop, value):
        theirs = dot(ps[loop, 1 - c], value, 1, 0)
        sb[k] = theirs.astype(BF).reshape(Q, 2, PAD, W)
        rs_twin(k).start()
        tb[k] = dot(ps[loop, c], value, 1, 0).astype(BF).reshape(Q, 2, PAD, W)

    def rs_spread(k):
        rs_twin(k).wait_recv()
        tb[k] = (tb[k].astype(F32) + sib[k].astype(F32)).astype(BF)
        each(Q, lambda i: rs_hop(k, i).start())

    def rs_gather(k):
        total = tb[k, q].astype(F32)
        for i in range(1, Q):
            rs_hop(k, i).wait_recv()
            total = total + rb[k, i].astype(F32)
        uf[k] = total
        ub[k] = uf[k, 1 - zh].astype(BF)
        rs_far(k).start()

    def rs_total(k):
        rs_far(k).wait_recv()

        def drain():
            rs_twin(k).wait_send()
            each(Q, lambda i: rs_hop(k, i).wait_send())
            rs_far(k).wait_send()

        pending.append(drain)
        return (uf[k, zh] + zb[k].astype(F32))[0:T]

    lanes = iota((T, 2 * MARKS), 1)
    named = jnp.zeros((T, 2 * MARKS), jnp.bool_)
    r0, r1 = routes_ref[0], routes_ref[1]
    for k in range(s.top):
        chosen = jnp.where(lanes < MARKS, r0[:, k : k + 1], r1[:, k : k + 1] + MARKS)
        named = named | (chosen == lanes)
    marks = jnp.where(named, 1.0, 0.0)
    earlier = jnp.zeros((T, 2 * MARKS), F32)
    t_of = iota((T, 2 * MARKS), 0)
    for t in range(T - 1):
        earlier = earlier + jnp.where(t_of > t, marks[t : t + 1], 0.0)
    ax[c, q, zh] = jnp.zeros((PAD, W + 2 * MARKS), BF)
    ax[c, q, zh, 0:T, 0:W] = x_ref[...]
    ax[c, q, zh, 0:T, W:] = (marks * (1.0 + earlier)).astype(BF)
    ag_start(0, ax)
    ac[c, q, zh] = jnp.zeros((PAD, W), BF)
    ac[c, q, zh, 0:T] = cot_ref[...]
    a1[c, q, zh] = jnp.zeros((PAD, W), BF)
    a2[c, q, zh] = jnp.zeros((PAD, W), BF)
    gain = gain_ref[...]
    sel_pick = jnp.where(iota((8, s.experts), 1) == e, 1.0, 0.0).astype(BF)
    sel_row = dot(sel_pick, sel_ref[...], 1, 1)

    ag_forward(0, ax)
    ag_start(1, ac)
    ag_join(0, ax)
    ag_finish(0, ax)

    def build(loop):
        n = 2 * half
        table = ax[:, :, :, :, W:].reshape(n, 2 * MARKS)
        mine = iota((8, 2 * MARKS), 1) == e + loop * MARKS
        wide = dot(jnp.where(mine, 1.0, 0.0).astype(BF), table, 1, 1)[0:1]
        wide_i = wide.astype(jnp.int32)
        row = jnp.where(wide_i > 0, 3 * (iota((1, n), 1) // PAD) + wide_i - 1, -1)
        pg[loop] = jnp.where(iota((R, n), 0) == row, 1.0, 0.0).astype(BF)
        picked = iota((n, 2 * MARKS), 1) == e + loop * MARKS
        tall = jnp.sum(jnp.where(picked, table.astype(F32), 0.0), axis=1, keepdims=True).astype(jnp.int32)
        place_ = jnp.where(tall > 0, 3 * (iota((n, 1), 0) // PAD) + tall - 1, -1)
        ps[loop] = (
            jnp.where(iota((n, R), 1) == place_, 1.0, 0.0).astype(BF).reshape(2, half, R)
        )

    def gathered(a):
        return a[:, :, :, :, 0:W].reshape(2 * half, W)

    def forward_in(loop, a):
        xr = dot(pg[loop], gathered(a), 1, 0)
        rows[loop] = xr.astype(BF)
        y = xr * gain
        yb = y.astype(BF)
        fs_fill(loop, dot(yb, up_ref[...], 1, 0))
        fs_start(loop)
        squares = dot(jnp.ones((8, W), F32), xr * xr, 1, 1, HIGHEST)
        logits = dot(sel_row, y, 1, 1, HIGHEST)
        ext_start(loop, two_rows(squares, logits))

    def forward_mid(loop):
        ext = ext_sum(loop)
        inv_l = lax.rsqrt(ext[0:1] / D + EPSILON)
        logit_l = ext[1:2] * inv_l
        gate_l = jax.nn.sigmoid(logit_l)
        inv, gate = column(inv_l), column(gate_l)
        pre = fs_sum(loop) * inv
        sig = jax.nn.sigmoid(pre)
        hid = (pre * sig).astype(BF)
        pre_k[loop] = pre
        slope_k[loop] = sig * (1.0 + pre * (1.0 - sig))
        hid_k[loop] = hid
        return SimpleNamespace(inv=inv, gate=gate, gate_l=gate_l, logit_l=logit_l, hid=hid)

    def forward_out(loop, st, k):
        out = dot(fg_value(loop), down_ref[...], 1, 0).astype(BF).astype(F32)
        rs_start(k, loop, (st.gate * out).astype(BF))

    def backward_in(loop, a):
        gr = dot(pg[loop], gathered(a), 1, 0).astype(BF)
        grads[loop] = gr
        fs_fill(2 + loop, dot(gr, down_ref[...], 1, 1))

    def backward_mid(loop, st):
        dh = dh_k[loop]
        hg = (st.gate * dh * slope_k[loop]).astype(BF)
        fg_start(2 + loop, hg)
        ones = jnp.ones((8, HL), F32)
        gg = dot(ones, hid_k[loop].astype(F32) * dh, 1, 1, HIGHEST)
        inner = dot(ones, hg.astype(F32) * pre_k[loop], 1, 1, HIGHEST)
        ext_start(2 + loop, two_rows(gg, inner))

    def backward_out(loop, st, k):
        ext = ext_sum(2 + loop)
        lgr_l = ext[0:1] * st.gate_l * (1.0 - st.gate_l)
        inner_l = ext[1:2] + lgr_l * st.logit_l
        lgr, inner = column(lgr_l), column(inner_l)
        fg_wait(2 + loop)
        bg = dot(fg_value(2 + loop), up_ref[...], 1, 1).astype(BF).astype(F32)
        xr = rows[loop].astype(F32)
        ng = bg + lgr * sel_row[0:1]
        contribution = st.inv * gain * ng - (st.inv * st.inv / D) * inner * xr
        rs_start(k, loop, contribution.astype(BF))
        return lgr_l

    def normed(loop, st):
        return (rows[loop].astype(F32) * st.inv * gain).astype(BF)

    def d_sent(loop, st):
        return (grads[loop].astype(F32) * st.gate).astype(BF)

    build(0)
    forward_in(0, ax)
    build(1)
    ag_forward(1, ac)
    ag_join(1, ac)
    ag_finish(1, ac)
    backward_in(1, ac)
    st0 = forward_mid(0)
    fg_start(0, st0.hid)
    fs_start(3)
    fg_wait(0)
    forward_out(0, st0, 0)
    rs_spread(0)
    dh_k[1] = fs_sum(3)
    rs_gather(0)
    x1 = (x_ref[...].astype(F32) + rs_total(0)).astype(BF)
    a1[c, q, zh, 0:T] = x1
    ag_start(2, a1)
    ag_forward(2, a1)
    ag_join(2, a1)
    ag_finish(2, a1)
    forward_in(1, a1)
    st1 = forward_mid(1)
    backward_mid(1, st1)
    fg_start(1, st1.hid)
    lgr1_l = backward_out(1, st1, 2)
    rs_spread(2)
    n1 = normed(1, st1)
    up_acc[...] = dot(n1, fg_value(3), 0, 0)
    rs_gather(2)
    fg_wait(1)
    down_acc[...] = dot(fg_value(1), d_sent(1, st1), 0, 0)
    sel_acc = dot(jnp.broadcast_to(lgr1_l, (8, R)), n1.astype(F32), 1, 0, HIGHEST)
    g1 = (cot_ref[...].astype(F32) + rs_total(2)).astype(BF)
    a2[c, q, zh, 0:T] = g1
    ag_start(3, a2)
    forward_out(1, st1, 1)
    ag_forward(3, a2)
    ag_join(3, a2)
    ag_finish(3, a2)
    backward_in(0, a2)
    fs_start(2)
    rs_spread(1)
    ddown_ref[...] = (down_acc[...] + dot(fg_value(0), d_sent(0, st0), 0, 0)).astype(BF)
    dh_k[0] = fs_sum(2)
    backward_mid(0, st0)
    rs_gather(1)
    lgr0_l = backward_out(0, st0, 3)
    n0 = normed(0, st0)
    sel_acc = sel_acc + dot(jnp.broadcast_to(lgr0_l, (8, R)), n0.astype(F32), 1, 0, HIGHEST)
    tile = jnp.zeros((8, 128), F32)
    for i in range(W // 128):
        tile = jnp.where(iota((8, 128), 0) == i, sel_acc[:, i * 128 : (i + 1) * 128], tile)
    asel[c, q, zh] = tile
    ag_start(4, asel)
    rs_spread(3)
    up0 = dot(n0, fg_value(2), 0, 0)
    dup_ref[...] = (up_acc[...] + up0).astype(BF)
    ag_forward(4, asel)
    rs_gather(3)
    mixed_ref[...] = (a1[c, q, zh, 0:T].astype(F32) + rs_total(1)).astype(BF)
    ag_join(4, asel)
    ag_finish(4, asel)
    dtok_ref[...] = (a2[c, q, zh, 0:T].astype(F32) + rs_total(3)).astype(BF)
    for i in range(W // 128):
        stack = asel[:, :, :, i, :].reshape(2, 2 * Q, 128)
        both = jnp.stack([stack[0], stack[1]], axis=1).reshape(4 * Q, 128)
        dsel_ref[i * 128 : (i + 1) * 128, :] = both.T
    for drain in pending:
        drain()


def shards(s, tokens, gain, w_sel, w_up, w_down, routes, cotangent):
    Q, F, R, W, H = s.chips, s.fsdp, s.rows, s.width, s.hidden
    HL = H // F
    VM, DMA = pltpu.VMEM, pltpu.SemaphoreType.DMA
    half = Q * 2 * PAD
    gather = lambda w, t=BF, r=PAD: VM((2, Q, 2, r, w), t)
    scratch = [
        gather(W + 2 * MARKS), gather(W), gather(W), gather(W), gather(128, F32, 8),
        VM((4, F, R, HL), BF), VM((4, F, R, HL), BF), VM((4, F, R, HL), BF),
        VM((4, F, 8, R), F32), VM((8, 128), F32),
        VM((4, Q, 2, PAD, W), BF), VM((4, Q, 2, PAD, W), BF), VM((4, Q, 2, PAD, W), BF), VM((4, Q, 2, PAD, W), BF),
        VM((4, 2, PAD, W), F32), VM((4, PAD, W), BF), VM((4, PAD, W), BF),
        VM((2, R, 2 * half), BF), VM((2, 2, half, R), BF),
        VM((2, R, HL), F32), VM((2, R, HL), F32), VM((2, R, HL), BF), VM((2, R, HL), F32),
        VM((2, R, W), BF), VM((2, R, W), BF), VM((W, H), F32), VM((H, W), F32),
        DMA((8, F)), DMA((8, F)), DMA((4, F)), DMA((4, F)),
        DMA((5, 2, Q)), DMA((5, 2, Q)), DMA((5,)), DMA((5,)), DMA((5,)), DMA((5,)),
        DMA((4, Q)), DMA((4, Q)), DMA((4,)), DMA((4,)), DMA((4,)), DMA((4,)),
    ]
    T = tokens.shape[0]
    out = pl.pallas_call(
        functools.partial(kernel, s),
        out_shape=(
            jax.ShapeDtypeStruct((T, W), BF),
            jax.ShapeDtypeStruct((T, W), BF),
            jax.ShapeDtypeStruct((W, H), BF),
            jax.ShapeDtypeStruct((H, W), BF),
            jax.ShapeDtypeStruct((W, s.experts), F32),
        ),
        in_specs=[pl.BlockSpec(memory_space=pltpu.VMEM)] * 7,
        out_specs=[pl.BlockSpec(memory_space=pltpu.VMEM)] * 5,
        scratch_shapes=scratch,
        compiler_params=pltpu.CompilerParams(
            collective_id=0, has_side_effects=True, vmem_limit_bytes=60 * 1024 * 1024
        ),
        cost_estimate=pl.CostEstimate(flops=6 * 10**9, bytes_accessed=5 * 2**20, transcendentals=10**5),
    )(tokens, cotangent, gain.reshape(1, W), w_sel, w_up[0], w_down[0], routes)
    mixed, d_tokens, d_up, d_down, d_sel = out
    return mixed, d_tokens, d_up[None], d_down[None], d_sel


def solution(mesh):
    n_expert, fsdp = mesh.shape["expert"], mesh.shape["fsdp"]

    def whole(tokens, gain, w_sel, w_up, w_down, routes, cotangent):
        s = SimpleNamespace(
            chips=n_expert // 4,
            fsdp=fsdp,
            tokens=tokens.shape[0] // n_expert,
            rows=n_expert * 3,
            width=tokens.shape[1] // fsdp,
            model=tokens.shape[1],
            hidden=w_up.shape[2],
            experts=w_sel.shape[1],
            top=routes.shape[2],
        )
        return jax.shard_map(
            functools.partial(shards, s),
            mesh=mesh,
            in_specs=(
                P("expert", "fsdp"),
                P("fsdp"),
                P("fsdp", None),
                P("expert", "fsdp", None),
                P("expert", None, "fsdp"),
                P(None, "expert", None),
                P("expert", "fsdp"),
            ),
            out_specs=(
                P("expert", "fsdp"),
                P("expert", "fsdp"),
                P("expert", "fsdp", None),
                P("expert", None, "fsdp"),
                P("fsdp", None),
            ),
            check_vma=False,
        )(tokens, gain, w_sel, w_up, w_down, routes, cotangent)

    return whole
```

```python
import functools
from types import SimpleNamespace

import jax
import jax.numpy as jnp
from jax import lax
from jax.experimental import pallas as pl
from jax.experimental.pallas import tpu as pltpu
from jax.sharding import PartitionSpec as P

EPSILON = 1e-06
HIGHEST = lax.Precision.HIGHEST
MESH = pl.DeviceIdType.MESH
BF, F32 = jnp.bfloat16, jnp.float32
PAD = 16
MARKS = 64
CHUNKS = 2


def iota(shape, dim):
    return lax.broadcasted_iota(jnp.int32, shape, dim)


def dot(a, b, ca, cb, precision=None):
    return lax.dot_general(
        a, b, (((ca,), (cb,)), ((), ())), precision=precision, preferred_element_type=F32
    )


def column(lanes):
    n = lanes.shape[1]
    return jnp.sum(jnp.where(iota((n, n), 0) == iota((n, n), 1), lanes, 0.0), axis=1, keepdims=True)


def two_rows(first, second):
    return jnp.where(iota(first.shape, 0) == 0, first, second)


def kernel(
    s,
    x_ref, cot_ref, gain_ref, sel_ref, up_ref, down_ref, routes_ref,
    mixed_ref, dtok_ref, dup_ref, ddown_ref, dsel_ref,
    ax, ac, a1, a2, asel,
    pbuf, nbuf, qbuf, rbuf, full, ebuf,
    sb, sib, tb, rb, ub, zb,
    pg, ps, pre_k, slope_k, hid_k, dh_k, rows, grads, up_acc, down_acc,
    fn_send, fn_recv, fs_send, fs_recv, fx_send, fx_recv,
    ag_send, ag_recv, az_send, az_recv, as_send, as_recv,
    rs_send, rs_recv, rz_send, rz_recv, rb_send, rb_recv,
):
    Q, F, R, W, H, D = s.chips, s.fsdp, s.rows, s.width, s.hidden, s.model
    T = s.tokens
    HL = H // F
    half = Q * 2 * PAD
    e, z = lax.axis_index("expert"), lax.axis_index("fsdp")
    q, zh, c = e // 4, (e // 2) % 2, e % 2

    def place(q_, zh_, c_):
        return (q_ * 4 + zh_ * 2 + c_, z)

    RC = R // CHUNKS
    par, m = z % 2, z // 2
    near = (e, z + 1 - 2 * par)

    def quad(i):
        return lax.rem(m + i, F // 2)

    far, twin = place(q, 1 - zh, c), place(q, zh, 1 - c)

    def chip(i):
        return lax.rem(q + i, Q)

    def line(i):
        return lax.rem(z + i, F)

    def copy(src, dst, send, recv, device):
        return pltpu.make_async_remote_copy(
            src_ref=src, dst_ref=dst, send_sem=send, recv_sem=recv, device_id=device, device_id_type=MESH
        )

    def each(count, fn):
        lax.fori_loop(1, count, lambda i, t: (fn(i), t)[1], 0)

    pending = []

    def settle():
        for drain in pending:
            drain()
        pending.clear()

    barrier = pltpu.get_barrier_semaphore()

    def greet(device):
        pl.semaphore_signal(barrier, inc=1, device_id=device, device_id_type=MESH)

    each(F, lambda i: greet((e, line(i))))
    each(Q, lambda i: greet(place(chip(i), zh, c)))
    greet(far)
    greet(twin)
    pl.semaphore_wait(barrier, F + Q)

    def ag_hop(k, a, wave, i):
        src = a.at[c, q, zh if wave == 0 else 1 - zh]
        return copy(src, src, ag_send.at[k, wave, i], ag_recv.at[k, wave, i], place(chip(i), zh, c))

    def ag_far(k, a):
        src = a.at[c, q, zh]
        return copy(src, src, az_send.at[k], az_recv.at[k], far)

    def ag_twin(k, a, i):
        src = a.at[c, lax.rem(q + Q - i, Q)]
        return copy(src, src, as_send.at[k, i], as_recv.at[k, i], twin)

    def ag_twin_wait(k, a):
        ag_twin(k, a, 0).wait_recv()
        each(Q, lambda i: ag_twin(k, a, i).wait_recv())

    def ag_twin_drain(k, a):
        ag_twin(k, a, 0).wait_send()
        each(Q, lambda i: ag_twin(k, a, i).wait_send())

    def ag_start(k, a):
        ag_far(k, a).start()
        each(Q, lambda i: ag_hop(k, a, 0, i).start())

    def ag_forward(k, a):
        ag_far(k, a).wait_recv()
        each(Q, lambda i: ag_hop(k, a, 1, i).start())
        ag_twin(k, a, 0).start()

    def ag_pair_hop(k, a, i):
        src = a.at[c, q]
        return copy(src, src, ag_send.at[k, 0, i], ag_recv.at[k, 0, i], place(chip(i), zh, c))

    def ag_pair(k, a):
        each(Q, lambda i: ag_pair_hop(k, a, i).start())
        ag_twin(k, a, 0).start()

    def ag_pair_join(k, a):
        def pass_on(i):
            ag_pair_hop(k, a, i).wait_recv()
            ag_twin(k, a, i).start()

        each(Q, pass_on)

    def ag_pair_finish(k, a):
        ag_twin_wait(k, a)

        def drain():
            each(Q, lambda i: ag_pair_hop(k, a, i).wait_send())
            ag_twin_drain(k, a)

        pending.append(drain)

    def ag_join(k, a):
        def pass_on(i):
            ag_hop(k, a, 0, i).wait_recv()
            ag_hop(k, a, 1, i).wait_recv()
            ag_twin(k, a, i).start()

        each(Q, pass_on)

    def ag_finish(k, a):
        ag_twin_wait(k, a)

        def drain():
            ag_far(k, a).wait_send()
            each(Q, lambda i: ag_hop(k, a, 0, i).wait_send())
            each(Q, lambda i: ag_hop(k, a, 1, i).wait_send())
            ag_twin_drain(k, a)

        pending.append(drain)

    def fs_near(k, p):
        src = pbuf.at[k, p, 1 - par]
        return copy(src, nbuf.at[k, p], fn_send.at[k, p], fn_recv.at[k, p], near)

    def fs_hop(k, p, i):
        src, dst = qbuf.at[k, p, quad(i)], rbuf.at[k, p, i]
        return copy(src, dst, fs_send.at[k, p, i], fs_recv.at[k, p, i], (e, 2 * quad(i) + par))

    def fs_ext(k, i):
        return copy(ebuf.at[k, 0], ebuf.at[k, i], fx_send.at[k, i], fx_recv.at[k, i], (e, line(i)))

    def fs_fill(k, part_of):
        for p in range(CHUNKS):
            value = part_of(slice(p * RC, (p + 1) * RC))
            for j in range(F):
                pbuf[k, p, j % 2, j // 2] = value[:, j * HL : (j + 1) * HL].astype(BF)
            fs_near(k, p).start()

    def fs_spread(k):
        for p in range(CHUNKS):
            fs_near(k, p).wait_recv()
            qbuf[k, p] = (pbuf[k, p, par].astype(F32) + nbuf[k, p].astype(F32)).astype(BF)
            each(F // 2, lambda i: fs_hop(k, p, i).start())

        def drain():
            for p in range(CHUNKS):
                fs_near(k, p).wait_send()
                each(F // 2, lambda i: fs_hop(k, p, i).wait_send())

        pending.append(drain)

    def fs_sum(k, p):
        total = qbuf[k, p, m].astype(F32)
        for i in range(1, F // 2):
            fs_hop(k, p, i).wait_recv()
            total = total + rbuf[k, p, i].astype(F32)
        return total

    def ext_start(k, value):
        ebuf[k, 0] = value
        each(F, lambda i: fs_ext(k, i).start())
        pending.append(lambda: each(F, lambda i: fs_ext(k, i).wait_send()))

    def ext_sum(k):
        total = ebuf[k, 0]
        for i in range(1, F):
            fs_ext(k, i).wait_recv()
            total = total + ebuf[k, i]
        return total

    def fg_hop(k, p, i):
        src = full.at[k, p, par, m]
        return copy(src, src, fs_send.at[4 + k, p, i], fs_recv.at[4 + k, p, i], (e, 2 * quad(i) + par))

    def fg_near(k, p):
        src = full.at[k, p, par]
        return copy(src, src, fn_send.at[4 + k, p], fn_recv.at[4 + k, p], near)

    def fg_start(k, p, value):
        full[k, p, par, m] = value
        each(F // 2, lambda i: fg_hop(k, p, i).start())

    def fg_forward(k):
        for p in range(CHUNKS):
            each(F // 2, lambda i: fg_hop(k, p, i).wait_recv())
            fg_near(k, p).start()

    def fg_wait(k):
        for p in range(CHUNKS):
            fg_near(k, p).wait_recv()

        def drain():
            for p in range(CHUNKS):
                fg_near(k, p).wait_send()
                each(F // 2, lambda i: fg_hop(k, p, i).wait_send())

        pending.append(drain)

    def fg_value(k):
        parts = [
            jnp.concatenate([full[k, p, j % 2, j // 2] for j in range(F)], axis=1) for p in range(CHUNKS)
        ]
        return jnp.concatenate(parts, axis=0)

    def rs_twin(k):
        return copy(sb.at[k], sib.at[k], rb_send.at[k], rb_recv.at[k], twin)

    def rs_hop(k, i):
        return copy(tb.at[k, chip(i)], rb.at[k, i], rs_send.at[k, i], rs_recv.at[k, i], place(chip(i), zh, c))

    def rs_far(k):
        if k % 2:
            return copy(ub.at[k, 1 - zh], zb.at[k, 1 - zh], rz_send.at[k], rz_recv.at[k], far)
        return copy(ub.at[k], zb.at[k], rz_send.at[k], rz_recv.at[k], far)

    def rs_start(k, loop, value):
        theirs = dot(ps[loop, 1 - c], value, 1, 0)
        sb[k] = theirs.astype(BF).reshape(Q, 2, PAD, W)
        rs_twin(k).start()
        tb[k] = dot(ps[loop, c], value, 1, 0).astype(BF).reshape(Q, 2, PAD, W)

    def rs_spread(k):
        rs_twin(k).wait_recv()
        tb[k] = (tb[k].astype(F32) + sib[k].astype(F32)).astype(BF)
        each(Q, lambda i: rs_hop(k, i).start())

    def rs_gather(k):
        total = tb[k, q].astype(F32)
        for i in range(1, Q):
            rs_hop(k, i).wait_recv()
            total = total + rb[k, i].astype(F32)
        ub[k] = total.astype(BF)
        rs_far(k).start()

    def rs_total(k):
        rs_far(k).wait_recv()

        def drain():
            rs_twin(k).wait_send()
            each(Q, lambda i: rs_hop(k, i).wait_send())
            rs_far(k).wait_send()

        pending.append(drain)
        if k % 2:
            return (ub[k, zh].astype(F32) + zb[k, zh].astype(F32))[0:T]
        return ub[k].astype(F32) + zb[k].astype(F32)

    lanes = iota((T, 2 * MARKS), 1)
    named = jnp.zeros((T, 2 * MARKS), jnp.bool_)
    unit = jnp.where(iota((T, T), 0) == iota((T, T), 1), 1.0, 0.0).astype(BF)
    r0, r1 = (dot(unit, routes_ref[i].astype(F32).astype(BF), 1, 1).astype(jnp.int32) for i in range(2))
    for k in range(s.top):
        chosen = jnp.where(lanes < MARKS, r0[:, k : k + 1], r1[:, k : k + 1] + MARKS)
        named = named | (chosen == lanes)
    marks = jnp.where(named, 1.0, 0.0)
    earlier = jnp.zeros((T, 2 * MARKS), F32)
    t_of = iota((T, 2 * MARKS), 0)
    for t in range(T - 1):
        earlier = earlier + jnp.where(t_of > t, marks[t : t + 1], 0.0)
    ax[c, q, zh] = jnp.zeros((PAD, W + 2 * MARKS), BF)
    ax[c, q, zh, 0:T, 0:W] = x_ref[...]
    ax[c, q, zh, 0:T, W:] = (marks * (1.0 + earlier)).astype(BF)
    ag_start(0, ax)
    ac[c, q, zh] = jnp.zeros((PAD, W), BF)
    ac[c, q, zh, 0:T] = cot_ref[...]
    gain = gain_ref[...]
    sel_pick = jnp.where(iota((8, s.experts), 1) == e, 1.0, 0.0).astype(BF)
    sel_row = dot(sel_pick, sel_ref[...], 1, 0)

    ag_forward(0, ax)
    ag_join(0, ax)
    ag_finish(0, ax)

    n = 2 * half

    def marks_table():
        return ax[:, :, :, :, W:].reshape(n, 2 * MARKS)

    def build_gather(loop):
        table = marks_table()
        mine = iota((8, 2 * MARKS), 1) == e + loop * MARKS
        wide = dot(jnp.where(mine, 1.0, 0.0).astype(BF), table, 1, 1)[0:1]
        wide_i = wide.astype(jnp.int32)
        row = jnp.where(wide_i > 0, 3 * (iota((1, n), 1) // PAD) + wide_i - 1, -1)
        pg[loop] = jnp.where(iota((R, n), 0) == row, 1.0, 0.0).astype(BF)

    def build_scatter(loop):
        table = marks_table()
        picked = iota((n, 2 * MARKS), 1) == e + loop * MARKS
        tall = jnp.sum(jnp.where(picked, table.astype(F32), 0.0), axis=1, keepdims=True).astype(jnp.int32)
        place_ = jnp.where(tall > 0, 3 * (iota((n, 1), 0) // PAD) + tall - 1, -1)
        ps[loop] = (
            jnp.where(iota((n, R), 1) == place_, 1.0, 0.0).astype(BF).reshape(2, half, R)
        )

    def gathered(a):
        return a[:, :, :, :, 0:W].reshape(2 * half, W)

    def forward_in(loop, a):
        xr = dot(pg[loop], gathered(a), 1, 0)
        rows[loop] = xr.astype(BF)
        y = xr * gain
        yb = y.astype(BF)
        fs_fill(loop, lambda part: dot(yb[part], up_ref[...], 1, 0))
        squares = dot(jnp.ones((8, W), F32), xr * xr, 1, 1, HIGHEST)
        logits = dot(sel_row, y, 1, 1, HIGHEST)
        ext_start(loop, two_rows(squares, logits))

    def forward_mid(loop):
        ext = ext_sum(loop)
        inv_l = lax.rsqrt(ext[0:1] / D + EPSILON)
        logit_l = ext[1:2] * inv_l
        gate_l = jax.nn.sigmoid(logit_l)
        inv, gate = column(inv_l), column(gate_l)
        st = SimpleNamespace(inv=inv, gate=gate, gate_l=gate_l, logit_l=logit_l)
        for p in range(CHUNKS):
            part = slice(p * RC, (p + 1) * RC)
            pre = fs_sum(loop, p) * inv[part]
            sig = jax.nn.sigmoid(pre)
            hid = (pre * sig).astype(BF)
            slope = sig * (1.0 + pre * (1.0 - sig))
            pre_k[loop, part] = pre
            slope_k[loop, part] = slope
            hid_k[loop, part] = hid
            if loop == 0:
                fg_start(0, p, hid)
            else:
                fg_start(3, p, (gate[part] * dh_k[1, part] * slope).astype(BF))
        return st

    def forward_out(loop, st, k):
        out = dot(fg_value(loop), down_ref[...], 1, 0).astype(BF).astype(F32)
        rs_start(k, loop, (st.gate * out).astype(BF))

    def backward_in(loop, a):
        gr = dot(pg[loop], gathered(a), 1, 0).astype(BF)
        grads[loop] = gr
        fs_fill(2 + loop, lambda part: dot(gr[part], down_ref[...], 1, 1))

    def backward_mid(loop, st):
        for p in range(CHUNKS):
            part = slice(p * RC, (p + 1) * RC)
            dh = fs_sum(2 + loop, p)
            dh_k[loop, part] = dh
            fg_start(2 + loop, p, (st.gate[part] * dh * slope_k[loop, part]).astype(BF))

    def backward_ext(loop, st):
        dh = dh_k[loop]
        hg = (st.gate * dh * slope_k[loop]).astype(BF)
        ones = jnp.ones((8, HL), F32)
        gg = dot(ones, hid_k[loop].astype(F32) * dh, 1, 1, HIGHEST)
        inner = dot(ones, hg.astype(F32) * pre_k[loop], 1, 1, HIGHEST)
        ext_start(2 + loop, two_rows(gg, inner))

    def backward_out(loop, st, k):
        ext = ext_sum(2 + loop)
        lgr_l = ext[0:1] * st.gate_l * (1.0 - st.gate_l)
        inner_l = ext[1:2] + lgr_l * st.logit_l
        lgr, inner = column(lgr_l), column(inner_l)
        fg_wait(2 + loop)
        bg = dot(fg_value(2 + loop), up_ref[...], 1, 1).astype(BF).astype(F32)
        xr = rows[loop].astype(F32)
        ng = bg + lgr * sel_row[0:1]
        contribution = st.inv * gain * ng - (st.inv * st.inv / D) * inner * xr
        rs_start(k, loop, contribution.astype(BF))
        return lgr_l

    def normed(loop, st):
        return (rows[loop].astype(F32) * st.inv * gain).astype(BF)

    def d_sent(loop, st):
        return (grads[loop].astype(F32) * st.gate).astype(BF)

    build_gather(0)
    forward_in(0, ax)
    ag_start(1, ac)
    build_scatter(0)
    build_gather(1)
    fs_spread(0)
    build_scatter(1)
    ag_forward(1, ac)
    st0 = forward_mid(0)
    ag_join(1, ac)
    fg_forward(0)
    ag_finish(1, ac)
    fg_wait(0)
    forward_out(0, st0, 0)
    rs_spread(0)
    backward_in(1, ac)
    rs_gather(0)
    fs_spread(3)
    both = ax[c, q, :, :, 0:W].astype(F32)
    a1[c, q] = (both + rs_total(0)).astype(BF)
    ag_pair(2, a1)
    for p in range(CHUNKS):
        dh_k[1, p * RC : (p + 1) * RC] = fs_sum(3, p)
    ag_pair_join(2, a1)
    ag_pair_finish(2, a1)
    forward_in(1, a1)
    settle()
    fs_spread(1)
    st1 = forward_mid(1)
    backward_ext(1, st1)
    fg_forward(3)
    lgr1_l = backward_out(1, st1, 2)
    for p in range(CHUNKS):
        fg_start(1, p, hid_k[1, p * RC : (p + 1) * RC])
    rs_spread(2)
    n1 = normed(1, st1)
    up_acc[...] = dot(n1, fg_value(3), 0, 0)
    fg_forward(1)
    rs_gather(2)
    sel_acc = dot(jnp.broadcast_to(lgr1_l, (8, R)), n1.astype(F32), 1, 0, HIGHEST)
    fg_wait(1)
    down_acc[...] = dot(fg_value(1), d_sent(1, st1), 0, 0)
    both = ac[c, q].astype(F32)
    a2[c, q] = (both + rs_total(2)).astype(BF)
    ag_pair(3, a2)
    forward_out(1, st1, 1)
    ag_pair_join(3, a2)
    ag_pair_finish(3, a2)
    backward_in(0, a2)
    settle()
    rs_spread(1)
    fs_spread(2)
    ddown_ref[...] = (down_acc[...] + dot(fg_value(0), d_sent(0, st0), 0, 0)).astype(BF)
    n0 = normed(0, st0)
    backward_mid(0, st0)
    backward_ext(0, st0)
    rs_gather(1)
    fg_forward(2)
    lgr0_l = backward_out(0, st0, 3)
    sel_acc = sel_acc + dot(jnp.broadcast_to(lgr0_l, (8, R)), n0.astype(F32), 1, 0, HIGHEST)
    tile = jnp.zeros((8, 128), F32)
    for i in range(W // 128):
        tile = jnp.where(iota((8, 128), 0) == i, sel_acc[:, i * 128 : (i + 1) * 128], tile)
    asel[c, q, zh] = tile
    ag_start(4, asel)
    rs_spread(3)
    settle()
    up0 = dot(n0, fg_value(2), 0, 0)
    dup_ref[...] = (up_acc[...] + up0).astype(BF)
    mixed_ref[...] = (a1[c, q, zh, 0:T].astype(F32) + rs_total(1)).astype(BF)
    ag_forward(4, asel)
    rs_gather(3)
    ag_join(4, asel)
    ag_finish(4, asel)
    for i in range(W // 128):
        stack = asel[:, :, :, i, :].reshape(2, 2 * Q, 128)
        dsel_ref[:, i * 128 : (i + 1) * 128] = jnp.stack([stack[0], stack[1]], axis=1).reshape(4 * Q, 128)
    dtok_ref[...] = (a2[c, q, zh, 0:T].astype(F32) + rs_total(3)).astype(BF)
    settle()


def shards(s, tokens, gain, w_sel, w_up, w_down, routes, cotangent):
    Q, F, R, W, H = s.chips, s.fsdp, s.rows, s.width, s.hidden
    HL, NC = H // F, CHUNKS
    RC = R // NC
    VM, DMA = pltpu.VMEM, pltpu.SemaphoreType.DMA
    half = Q * 2 * PAD
    gather = lambda w, t=BF, r=PAD: VM((2, Q, 2, r, w), t)
    scratch = [
        gather(W + 2 * MARKS), gather(W), gather(W), gather(W), gather(128, F32, 8),
        VM((4, NC, 2, F // 2, RC, HL), BF), VM((4, NC, F // 2, RC, HL), BF), VM((4, NC, F // 2, RC, HL), BF),
        VM((4, NC, F // 2, RC, HL), BF), VM((4, NC, 2, F // 2, RC, HL), BF), VM((4, F, 8, R), F32),
        VM((4, Q, 2, PAD, W), BF), VM((4, Q, 2, PAD, W), BF), VM((4, Q, 2, PAD, W), BF), VM((4, Q, 2, PAD, W), BF),
        VM((4, 2, PAD, W), BF), VM((4, 2, PAD, W), BF),
        VM((2, R, 2 * half), BF), VM((2, 2, half, R), BF),
        VM((2, R, HL), F32), VM((2, R, HL), F32), VM((2, R, HL), BF), VM((2, R, HL), F32),
        VM((2, R, W), BF), VM((2, R, W), BF), VM((W, H), F32), VM((H, W), F32),
        DMA((8, NC)), DMA((8, NC)), DMA((8, NC, F // 2)), DMA((8, NC, F // 2)), DMA((4, F)), DMA((4, F)),
        DMA((5, 2, Q)), DMA((5, 2, Q)), DMA((5,)), DMA((5,)), DMA((5, Q)), DMA((5, Q)),
        DMA((4, Q)), DMA((4, Q)), DMA((4,)), DMA((4,)), DMA((4,)), DMA((4,)),
    ]
    T = tokens.shape[0]
    out = pl.pallas_call(
        functools.partial(kernel, s),
        out_shape=(
            jax.ShapeDtypeStruct((T, W), BF),
            jax.ShapeDtypeStruct((T, W), BF),
            jax.ShapeDtypeStruct((W, H), BF),
            jax.ShapeDtypeStruct((H, W), BF),
            jax.ShapeDtypeStruct((s.experts, W), F32),
        ),
        in_specs=[pl.BlockSpec(memory_space=pltpu.VMEM)] * 7,
        out_specs=[pl.BlockSpec(memory_space=pltpu.VMEM)] * 5,
        scratch_shapes=scratch,
        compiler_params=pltpu.CompilerParams(
            collective_id=0, has_side_effects=True, vmem_limit_bytes=60 * 1024 * 1024
        ),
        cost_estimate=pl.CostEstimate(flops=6 * 10**9, bytes_accessed=5 * 2**20, transcendentals=10**5),
    )(tokens, cotangent, gain.reshape(1, W), w_sel.T, w_up[0], w_down[0], routes.swapaxes(1, 2))
    mixed, d_tokens, d_up, d_down, d_sel = out
    return mixed, d_tokens, d_up[None], d_down[None], d_sel.T


def solution(mesh):
    n_expert, fsdp = mesh.shape["expert"], mesh.shape["fsdp"]

    def whole(tokens, gain, w_sel, w_up, w_down, routes, cotangent):
        s = SimpleNamespace(
            chips=n_expert // 4,
            fsdp=fsdp,
            tokens=tokens.shape[0] // n_expert,
            rows=n_expert * 3,
            width=tokens.shape[1] // fsdp,
            model=tokens.shape[1],
            hidden=w_up.shape[2],
            experts=w_sel.shape[1],
            top=routes.shape[2],
        )
        return jax.shard_map(
            functools.partial(shards, s),
            mesh=mesh,
            in_specs=(
                P("expert", "fsdp"),
                P("fsdp"),
                P("fsdp", None),
                P("expert", "fsdp", None),
                P("expert", None, "fsdp"),
                P(None, "expert", None),
                P("expert", "fsdp"),
            ),
            out_specs=(
                P("expert", "fsdp"),
                P("expert", "fsdp"),
                P("expert", "fsdp", None),
                P("expert", None, "fsdp"),
                P("fsdp", None),
            ),
            check_vma=False,
        )(tokens, gain, w_sel, w_up, w_down, routes, cotangent)

    return whole
```

```python
import functools
from types import SimpleNamespace

import jax
import jax.numpy as jnp
from jax import lax
from jax.experimental import pallas as pl
from jax.experimental.pallas import tpu as pltpu
from jax.sharding import PartitionSpec as P

EPSILON = 1e-06
MESH = pl.DeviceIdType.MESH
BF, F32 = jnp.bfloat16, jnp.float32
PAD = 16
MARKS = 64
CHUNKS = 3


def iota(shape, dim):
    return lax.broadcasted_iota(jnp.int32, shape, dim)


def dot(a, b, ca, cb):
    return lax.dot_general(a, b, (((ca,), (cb,)), ((), ())), preferred_element_type=F32)


def column(lanes):
    n = lanes.shape[1]
    return jnp.sum(jnp.where(iota((n, n), 0) == iota((n, n), 1), lanes, 0.0), axis=1, keepdims=True)


def two_rows(first, second):
    return jnp.where(iota(first.shape, 0) == 0, first, second)


def kernel(
    s,
    x_ref, cot_ref, gain_ref, sel_ref, up_hbm, down_hbm, routes_ref,
    mixed_ref, dtok_ref, dup_hbm, ddown_hbm, dsel_ref,
    up_ref, down_ref, dup_ref, ddown_ref, own_sem,
    ax, ac, a1, a2, asel,
    pbuf, nbuf, qbuf, rbuf, full, ebuf,
    sb, sib, tb, rb, ub, zb,
    pg, ps, pre_k, slope_k, hid_k, dh_k, rows, grads, up_acc, down_acc,
    fn_send, fn_recv, fs_send, fs_recv, fx_send, fx_recv,
    ag_send, ag_recv, az_send, az_recv, as_send, as_recv,
    rs_send, rs_recv, rz_send, rz_recv, rb_send, rb_recv,
):
    Q, F, R, W, H, D = s.chips, s.fsdp, s.rows, s.width, s.hidden, s.model
    T = s.tokens
    HL = H // F
    half = Q * 2 * PAD
    e, z = lax.axis_index("expert"), lax.axis_index("fsdp")
    q, zh, c = e // 4, (e // 2) % 2, e % 2

    def place(q_, zh_, c_):
        return (q_ * 4 + zh_ * 2 + c_, z)

    RC = R // CHUNKS
    par, m = z % 2, z // 2
    near = (e, z + 1 - 2 * par)

    def quad(i):
        return lax.rem(m + i, F // 2)

    far, twin = place(q, 1 - zh, c), place(q, zh, 1 - c)

    def chip(i):
        return lax.rem(q + i, Q)

    def line(i):
        return lax.rem(z + i, F)

    def copy(src, dst, send, recv, device):
        return pltpu.make_async_remote_copy(
            src_ref=src, dst_ref=dst, send_sem=send, recv_sem=recv, device_id=device, device_id_type=MESH
        )

    def each(count, fn):
        lax.fori_loop(1, count, lambda i, t: (fn(i), t)[1], 0)

    def arrived(ref, sem):
        pltpu.make_async_copy(ref, ref, sem).wait()

    pending = []

    def settle():
        for drain in pending:
            drain()
        pending.clear()

    up_in = pltpu.make_async_copy(up_hbm, up_ref, own_sem.at[0])
    down_in = pltpu.make_async_copy(down_hbm, down_ref, own_sem.at[1])
    dup_out = pltpu.make_async_copy(dup_ref, dup_hbm, own_sem.at[2])
    ddown_out = pltpu.make_async_copy(ddown_ref, ddown_hbm, own_sem.at[3])
    up_in.start()
    down_in.start()
    barrier = pltpu.get_barrier_semaphore()

    def greet(device):
        pl.semaphore_signal(barrier, inc=1, device_id=device, device_id_type=MESH)

    each(F, lambda i: greet((e, line(i))))
    each(Q, lambda i: greet(place(chip(i), zh, c)))
    greet(far)
    greet(twin)
    pl.semaphore_wait(barrier, F + Q)

    def ag_hop(k, a, wave, i):
        src = a.at[c, q, zh if wave == 0 else 1 - zh]
        return copy(src, src, ag_send.at[k, wave], ag_recv.at[k, wave], place(chip(i), zh, c))

    def ag_far(k, a):
        src = a.at[c, q, zh]
        return copy(src, src, az_send.at[k], az_recv.at[k], far)

    def ag_twin(k, a):
        return copy(a.at[c], a.at[c], as_send.at[k], as_recv.at[k], twin)

    def ag_start(k, a):
        ag_far(k, a).start()
        each(Q, lambda i: ag_hop(k, a, 0, i).start())

    def ag_forward(k, a):
        ag_far(k, a).wait_recv()
        each(Q, lambda i: ag_hop(k, a, 1, i).start())

    def ag_join(k, a):
        arrived(a.at[c, pl.ds(0, Q - 1), 0], ag_recv.at[k, 0])
        arrived(a.at[c, pl.ds(0, Q - 1), 1], ag_recv.at[k, 1])
        ag_twin(k, a).start()

    def ag_finish(k, a):
        ag_twin(k, a).wait_recv()

        def drain():
            ag_far(k, a).wait_send()
            arrived(a.at[c, pl.ds(0, Q - 1), 0], ag_send.at[k, 0])
            arrived(a.at[c, pl.ds(0, Q - 1), 1], ag_send.at[k, 1])
            ag_twin(k, a).wait_send()

        pending.append(drain)

    def ag_pair_hop(k, a, i):
        src = a.at[c, q]
        return copy(src, src, ag_send.at[k, 0], ag_recv.at[k, 0], place(chip(i), zh, c))

    def ag_pair(k, a):
        each(Q, lambda i: ag_pair_hop(k, a, i).start())

    def ag_pair_join(k, a):
        arrived(a.at[c, pl.ds(0, Q - 1)], ag_recv.at[k, 0])
        ag_twin(k, a).start()

    def ag_pair_finish(k, a):
        ag_twin(k, a).wait_recv()

        def drain():
            arrived(a.at[c, pl.ds(0, Q - 1)], ag_send.at[k, 0])
            ag_twin(k, a).wait_send()

        pending.append(drain)

    def fs_near(k, p):
        src = pbuf.at[k, p, 1 - par]
        return copy(src, nbuf.at[k, p], fn_send.at[k, p], fn_recv.at[k, p], near)

    def fs_hop(k, p, i):
        src, dst = qbuf.at[k, p, quad(i)], rbuf.at[k, p, i]
        return copy(src, dst, fs_send.at[k, p], fs_recv.at[k, p], (e, 2 * quad(i) + par))

    def fs_ext(k, i):
        return copy(ebuf.at[k, 0], ebuf.at[k, i], fx_send.at[k], fx_recv.at[k], (e, line(i)))

    def fs_fill(k, part_of):
        for p in range(CHUNKS):
            value = part_of(slice(p * RC, (p + 1) * RC))
            for j in range(F):
                pbuf[k, p, j % 2, j // 2] = value[:, j * HL : (j + 1) * HL].astype(BF)
            fs_near(k, p).start()

    def fs_spread(k):
        for p in range(CHUNKS):
            fs_near(k, p).wait_recv()
            qbuf[k, p] = (pbuf[k, p, par].astype(F32) + nbuf[k, p].astype(F32)).astype(BF)
            each(F // 2, lambda i: fs_hop(k, p, i).start())

        def drain():
            for p in range(CHUNKS):
                fs_near(k, p).wait_send()
                arrived(rbuf.at[k, p, pl.ds(1, F // 2 - 1)], fs_send.at[k, p])

        pending.append(drain)

    def fs_sum(k, p):
        arrived(rbuf.at[k, p, pl.ds(1, F // 2 - 1)], fs_recv.at[k, p])
        total = qbuf[k, p, m].astype(F32)
        for i in range(1, F // 2):
            total = total + rbuf[k, p, i].astype(F32)
        return total

    def ext_start(k, value):
        ebuf[k, 0] = value
        each(F, lambda i: fs_ext(k, i).start())
        pending.append(lambda: arrived(ebuf.at[k, pl.ds(1, F - 1)], fx_send.at[k]))

    def ext_sum(k):
        arrived(ebuf.at[k, pl.ds(1, F - 1)], fx_recv.at[k])
        total = ebuf[k, 0]
        for i in range(1, F):
            total = total + ebuf[k, i]
        return total

    def fg_hop(k, p, i):
        src = full.at[k, p, par, m]
        return copy(src, src, fs_send.at[4 + k, p], fs_recv.at[4 + k, p], (e, 2 * quad(i) + par))

    def fg_near(k, p):
        src = full.at[k, p, par]
        return copy(src, src, fn_send.at[4 + k, p], fn_recv.at[4 + k, p], near)

    def fg_start(k, p, value):
        full[k, p, par, m] = value
        each(F // 2, lambda i: fg_hop(k, p, i).start())

    def fg_forward(k):
        for p in range(CHUNKS):
            arrived(full.at[k, p, par, pl.ds(0, F // 2 - 1)], fs_recv.at[4 + k, p])
            fg_near(k, p).start()

    def fg_wait(k):
        for p in range(CHUNKS):
            fg_near(k, p).wait_recv()

        def drain():
            for p in range(CHUNKS):
                fg_near(k, p).wait_send()
                arrived(full.at[k, p, par, pl.ds(0, F // 2 - 1)], fs_send.at[4 + k, p])

        pending.append(drain)

    def fg_value(k):
        parts = [
            jnp.concatenate([full[k, p, j % 2, j // 2] for j in range(F)], axis=1) for p in range(CHUNKS)
        ]
        return jnp.concatenate(parts, axis=0)

    def rs_twin(k):
        return copy(sb.at[k], sib.at[k], rb_send.at[k], rb_recv.at[k], twin)

    def rs_hop(k, i):
        return copy(tb.at[k, chip(i)], rb.at[k, i], rs_send.at[k], rs_recv.at[k], place(chip(i), zh, c))

    def rs_far(k):
        if k % 2:
            return copy(ub.at[k, 1 - zh], zb.at[k, 1 - zh], rz_send.at[k], rz_recv.at[k], far)
        return copy(ub.at[k], zb.at[k], rz_send.at[k], rz_recv.at[k], far)

    def rs_start(k, loop, value):
        theirs = dot(ps[loop, 1 - c], value, 1, 0)
        sb[k] = theirs.astype(BF).reshape(Q, 2, PAD, W)
        rs_twin(k).start()
        tb[k] = dot(ps[loop, c], value, 1, 0).astype(BF).reshape(Q, 2, PAD, W)

    def rs_spread(k):
        rs_twin(k).wait_recv()
        tb[k] = (tb[k].astype(F32) + sib[k].astype(F32)).astype(BF)
        each(Q, lambda i: rs_hop(k, i).start())

    def rs_gather(k):
        arrived(rb.at[k, pl.ds(1, Q - 1)], rs_recv.at[k])
        total = tb[k, q].astype(F32)
        for i in range(1, Q):
            total = total + rb[k, i].astype(F32)
        ub[k] = total.astype(BF)
        rs_far(k).start()

    def rs_total(k):
        rs_far(k).wait_recv()

        def drain():
            rs_twin(k).wait_send()
            arrived(rb.at[k, pl.ds(1, Q - 1)], rs_send.at[k])
            rs_far(k).wait_send()

        pending.append(drain)
        if k % 2:
            return (ub[k, zh].astype(F32) + zb[k, zh].astype(F32))[0:T]
        return ub[k].astype(F32) + zb[k].astype(F32)

    lanes = iota((T, 2 * MARKS), 1)
    named = jnp.zeros((T, 2 * MARKS), jnp.bool_)
    unit = jnp.where(iota((T, T), 0) == iota((T, T), 1), 1.0, 0.0).astype(BF)
    r0, r1 = (dot(unit, routes_ref[i].astype(F32).astype(BF), 1, 1).astype(jnp.int32) for i in range(2))
    for k in range(s.top):
        chosen = jnp.where(lanes < MARKS, r0[:, k : k + 1], r1[:, k : k + 1] + MARKS)
        named = named | (chosen == lanes)
    marks = jnp.where(named, 1.0, 0.0)
    earlier = jnp.zeros((T, 2 * MARKS), F32)
    t_of = iota((T, 2 * MARKS), 0)
    for t in range(T - 1):
        earlier = earlier + jnp.where(t_of > t, marks[t : t + 1], 0.0)
    ax[c, q, zh] = jnp.zeros((PAD, W + 2 * MARKS), BF)
    ax[c, q, zh, 0:T, 0:W] = x_ref[...]
    ax[c, q, zh, 0:T, W:] = (marks * (1.0 + earlier)).astype(BF)
    ag_start(0, ax)
    ac[c, q, zh] = jnp.zeros((PAD, W), BF)
    ac[c, q, zh, 0:T] = cot_ref[...]
    gain = gain_ref[...]
    sel_pick = jnp.where(iota((8, s.experts), 1) == e, 1.0, 0.0).astype(BF)
    sel_row = dot(sel_pick, sel_ref[...], 1, 0)

    ag_forward(0, ax)
    ag_join(0, ax)
    ag_finish(0, ax)

    n = 2 * half

    def marks_table():
        return ax[:, :, :, :, W:].reshape(n, 2 * MARKS)

    def build_gather(loop):
        table = marks_table()
        mine = iota((8, 2 * MARKS), 1) == e + loop * MARKS
        wide = dot(jnp.where(mine, 1.0, 0.0).astype(BF), table, 1, 1)[0:1]
        wide_i = wide.astype(jnp.int32)
        row = jnp.where(wide_i > 0, 3 * (iota((1, n), 1) // PAD) + wide_i - 1, -1)
        pg[loop] = jnp.where(iota((R, n), 0) == row, 1.0, 0.0).astype(BF)

    def build_scatter(loop):
        table = marks_table()
        picked = iota((n, 2 * MARKS), 1) == e + loop * MARKS
        tall = jnp.sum(jnp.where(picked, table.astype(F32), 0.0), axis=1, keepdims=True).astype(jnp.int32)
        place_ = jnp.where(tall > 0, 3 * (iota((n, 1), 0) // PAD) + tall - 1, -1)
        ps[loop] = (
            jnp.where(iota((n, R), 1) == place_, 1.0, 0.0).astype(BF).reshape(2, half, R)
        )

    def gathered(a):
        return a[:, :, :, :, 0:W].reshape(2 * half, W)

    def forward_in(loop, a):
        xr = dot(pg[loop], gathered(a), 1, 0)
        rows[loop] = xr.astype(BF)
        y = xr * gain
        yb = y.astype(BF)
        fs_fill(loop, lambda part: dot(yb[part], up_ref[...], 1, 0))
        squares = dot(jnp.ones((8, W), BF), (xr * xr).astype(BF), 1, 1)
        logits = dot(sel_row.astype(BF), yb, 1, 1)
        ext_start(loop, two_rows(squares, logits))

    def forward_mid(loop):
        ext = ext_sum(loop)
        inv_l = lax.rsqrt(ext[0:1] / D + EPSILON)
        logit_l = ext[1:2] * inv_l
        gate_l = jax.nn.sigmoid(logit_l)
        inv, gate = column(inv_l), column(gate_l)
        st = SimpleNamespace(inv=inv, gate=gate, gate_l=gate_l, logit_l=logit_l)
        for p in range(CHUNKS):
            part = slice(p * RC, (p + 1) * RC)
            pre = fs_sum(loop, p) * inv[part]
            sig = jax.nn.sigmoid(pre)
            hid = (pre * sig).astype(BF)
            slope = sig * (1.0 + pre * (1.0 - sig))
            pre_k[loop, part] = pre
            slope_k[loop, part] = slope
            hid_k[loop, part] = hid
            if loop == 0:
                fg_start(0, p, hid)
            else:
                fg_start(3, p, (gate[part] * dh_k[1, part] * slope).astype(BF))
        return st

    def forward_out(loop, st, k):
        out = dot(fg_value(loop), down_ref[...], 1, 0).astype(BF).astype(F32)
        rs_start(k, loop, (st.gate * out).astype(BF))

    def backward_in(loop, a):
        gr = dot(pg[loop], gathered(a), 1, 0).astype(BF)
        grads[loop] = gr
        fs_fill(2 + loop, lambda part: dot(gr[part], down_ref[...], 1, 1))

    def backward_mid(loop, st):
        for p in range(CHUNKS):
            part = slice(p * RC, (p + 1) * RC)
            dh = fs_sum(2 + loop, p)
            dh_k[loop, part] = dh
            fg_start(2 + loop, p, (st.gate[part] * dh * slope_k[loop, part]).astype(BF))

    def backward_ext(loop, st):
        dh = dh_k[loop]
        hg = (st.gate * dh * slope_k[loop]).astype(BF)
        ones = jnp.ones((8, HL), BF)
        gg = dot(ones, (hid_k[loop].astype(F32) * dh).astype(BF), 1, 1)
        inner = dot(ones, (hg.astype(F32) * pre_k[loop]).astype(BF), 1, 1)
        ext_start(2 + loop, two_rows(gg, inner))

    def backward_out(loop, st, k):
        ext = ext_sum(2 + loop)
        lgr_l = ext[0:1] * st.gate_l * (1.0 - st.gate_l)
        inner_l = ext[1:2] + lgr_l * st.logit_l
        lgr, inner = column(lgr_l), column(inner_l)
        fg_wait(2 + loop)
        bg = dot(fg_value(2 + loop), up_ref[...], 1, 1).astype(BF).astype(F32)
        xr = rows[loop].astype(F32)
        ng = bg + lgr * sel_row[0:1]
        contribution = st.inv * gain * ng - (st.inv * st.inv / D) * inner * xr
        rs_start(k, loop, contribution.astype(BF))
        return lgr_l

    def normed(loop, st):
        return (rows[loop].astype(F32) * st.inv * gain).astype(BF)

    def d_sent(loop, st):
        return (grads[loop].astype(F32) * st.gate).astype(BF)

    build_gather(0)
    up_in.wait()
    forward_in(0, ax)
    ag_start(1, ac)
    build_scatter(0)
    build_gather(1)
    fs_spread(0)
    build_scatter(1)
    ag_forward(1, ac)
    st0 = forward_mid(0)
    ag_join(1, ac)
    fg_forward(0)
    ag_finish(1, ac)
    fg_wait(0)
    down_in.wait()
    forward_out(0, st0, 0)
    rs_spread(0)
    backward_in(1, ac)
    rs_gather(0)
    fs_spread(3)
    both = ax[c, q, :, :, 0:W].astype(F32)
    a1[c, q] = (both + rs_total(0)).astype(BF)
    ag_pair(2, a1)
    for p in range(CHUNKS):
        dh_k[1, p * RC : (p + 1) * RC] = fs_sum(3, p)
    ag_pair_join(2, a1)
    ag_pair_finish(2, a1)
    forward_in(1, a1)
    settle()
    fs_spread(1)
    st1 = forward_mid(1)
    backward_ext(1, st1)
    fg_forward(3)
    lgr1_l = backward_out(1, st1, 2)
    for p in range(CHUNKS):
        fg_start(1, p, hid_k[1, p * RC : (p + 1) * RC])
    rs_spread(2)
    n1 = normed(1, st1)
    up_acc[...] = dot(n1, fg_value(3), 0, 0)
    fg_forward(1)
    rs_gather(2)
    sel_acc = dot(jnp.broadcast_to(lgr1_l, (8, R)).astype(BF), n1, 1, 0)
    fg_wait(1)
    down_acc[...] = dot(fg_value(1), d_sent(1, st1), 0, 0)
    both = ac[c, q].astype(F32)
    a2[c, q] = (both + rs_total(2)).astype(BF)
    ag_pair(3, a2)
    forward_out(1, st1, 1)
    ag_pair_join(3, a2)
    ag_pair_finish(3, a2)
    backward_in(0, a2)
    settle()
    rs_spread(1)
    fs_spread(2)
    ddown_ref[...] = (down_acc[...] + dot(fg_value(0), d_sent(0, st0), 0, 0)).astype(BF)
    ddown_out.start()
    n0 = normed(0, st0)
    backward_mid(0, st0)
    backward_ext(0, st0)
    rs_gather(1)
    fg_forward(2)
    lgr0_l = backward_out(0, st0, 3)
    rs_spread(3)
    sel_acc = sel_acc + dot(jnp.broadcast_to(lgr0_l, (8, R)).astype(BF), n0, 1, 0)
    tile = jnp.zeros((8, 128), F32)
    for i in range(W // 128):
        tile = jnp.where(iota((8, 128), 0) == i, sel_acc[:, i * 128 : (i + 1) * 128], tile)
    asel[c, q, zh] = tile
    ag_start(4, asel)
    settle()
    up0 = dot(n0, fg_value(2), 0, 0)
    dup_ref[...] = (up_acc[...] + up0).astype(BF)
    dup_out.start()
    mixed_ref[...] = (a1[c, q, zh, 0:T].astype(F32) + rs_total(1)).astype(BF)
    ag_forward(4, asel)
    rs_gather(3)
    ag_join(4, asel)
    ag_finish(4, asel)
    for i in range(W // 128):
        stack = asel[:, :, :, i, :].reshape(2, 2 * Q, 128)
        dsel_ref[:, i * 128 : (i + 1) * 128] = jnp.stack([stack[0], stack[1]], axis=1).reshape(4 * Q, 128)
    dtok_ref[...] = (a2[c, q, zh, 0:T].astype(F32) + rs_total(3)).astype(BF)
    dup_out.wait()
    ddown_out.wait()
    settle()


def shards(s, tokens, gain, w_sel, w_up, w_down, routes, cotangent):
    Q, F, R, W, H = s.chips, s.fsdp, s.rows, s.width, s.hidden
    HL, NC = H // F, CHUNKS
    RC = R // NC
    VM, DMA = pltpu.VMEM, pltpu.SemaphoreType.DMA
    half = Q * 2 * PAD
    gather = lambda w, t=BF, r=PAD: VM((2, Q, 2, r, w), t)
    scratch = [
        VM((W, H), BF), VM((H, W), BF), VM((W, H), BF), VM((H, W), BF), DMA((4,)),
        gather(W + 2 * MARKS), gather(W), gather(W), gather(W), gather(128, F32, 8),
        VM((4, NC, 2, F // 2, RC, HL), BF), VM((4, NC, F // 2, RC, HL), BF), VM((4, NC, F // 2, RC, HL), BF),
        VM((4, NC, F // 2, RC, HL), BF), VM((4, NC, 2, F // 2, RC, HL), BF), VM((4, F, 8, R), F32),
        VM((4, Q, 2, PAD, W), BF), VM((4, Q, 2, PAD, W), BF), VM((4, Q, 2, PAD, W), BF), VM((4, Q, 2, PAD, W), BF),
        VM((4, 2, PAD, W), BF), VM((4, 2, PAD, W), BF),
        VM((2, R, 2 * half), BF), VM((2, 2, half, R), BF),
        VM((2, R, HL), F32), VM((2, R, HL), F32), VM((2, R, HL), BF), VM((2, R, HL), F32),
        VM((2, R, W), BF), VM((2, R, W), BF), VM((W, H), F32), VM((H, W), F32),
        DMA((8, NC)), DMA((8, NC)), DMA((8, NC)), DMA((8, NC)), DMA((4,)), DMA((4,)),
        DMA((5, 2)), DMA((5, 2)), DMA((5,)), DMA((5,)), DMA((5,)), DMA((5,)),
        DMA((4,)), DMA((4,)), DMA((4,)), DMA((4,)), DMA((4,)), DMA((4,)),
    ]
    T = tokens.shape[0]
    vmem, hbm = pl.BlockSpec(memory_space=pltpu.VMEM), pl.BlockSpec(memory_space=pl.ANY)
    out = pl.pallas_call(
        functools.partial(kernel, s),
        out_shape=(
            jax.ShapeDtypeStruct((T, W), BF),
            jax.ShapeDtypeStruct((T, W), BF),
            jax.ShapeDtypeStruct((W, H), BF),
            jax.ShapeDtypeStruct((H, W), BF),
            jax.ShapeDtypeStruct((s.experts, W), F32),
        ),
        in_specs=[vmem] * 4 + [hbm] * 2 + [vmem],
        out_specs=[vmem] * 2 + [hbm] * 2 + [vmem],
        scratch_shapes=scratch,
        compiler_params=pltpu.CompilerParams(
            collective_id=0, has_side_effects=True, vmem_limit_bytes=60 * 1024 * 1024
        ),
        cost_estimate=pl.CostEstimate(flops=6 * 10**9, bytes_accessed=5 * 2**20, transcendentals=10**5),
    )(tokens, cotangent, gain.reshape(1, W), w_sel.T, w_up[0], w_down[0], routes.swapaxes(1, 2))
    mixed, d_tokens, d_up, d_down, d_sel = out
    return mixed, d_tokens, d_up[None], d_down[None], d_sel.T


def solution(mesh):
    n_expert, fsdp = mesh.shape["expert"], mesh.shape["fsdp"]

    def whole(tokens, gain, w_sel, w_up, w_down, routes, cotangent):
        s = SimpleNamespace(
            chips=n_expert // 4,
            fsdp=fsdp,
            tokens=tokens.shape[0] // n_expert,
            rows=n_expert * 3,
            width=tokens.shape[1] // fsdp,
            model=tokens.shape[1],
            hidden=w_up.shape[2],
            experts=w_sel.shape[1],
            top=routes.shape[2],
        )
        return jax.shard_map(
            functools.partial(shards, s),
            mesh=mesh,
            in_specs=(
                P("expert", "fsdp"),
                P("fsdp"),
                P("fsdp", None),
                P("expert", "fsdp", None),
                P("expert", None, "fsdp"),
                P(None, "expert", None),
                P("expert", "fsdp"),
            ),
            out_specs=(
                P("expert", "fsdp"),
                P("expert", "fsdp"),
                P("expert", "fsdp", None),
                P("expert", None, "fsdp"),
                P("fsdp", None),
            ),
            check_vma=False,
        )(tokens, gain, w_sel, w_up, w_down, routes, cotangent)

    return whole
```

```python
import functools
from types import SimpleNamespace

import jax
import jax.numpy as jnp
from jax import lax
from jax.experimental import pallas as pl
from jax.experimental.pallas import tpu as pltpu
from jax.sharding import PartitionSpec as P

EPSILON = 1e-06
MESH = pl.DeviceIdType.MESH
BF, F32 = jnp.bfloat16, jnp.float32
PAD = 16
MARKS = 64
CHUNKS = 4


def iota(shape, dim):
    return lax.broadcasted_iota(jnp.int32, shape, dim)


def dot(a, b, ca, cb):
    return lax.dot_general(a, b, (((ca,), (cb,)), ((), ())), preferred_element_type=F32)


def column(lanes):
    n = lanes.shape[1]
    return jnp.sum(jnp.where(iota((n, n), 0) == iota((n, n), 1), lanes, 0.0), axis=1, keepdims=True)


def two_rows(first, second):
    return jnp.where(iota(first.shape, 0) == 0, first, second)


def kernel(
    s,
    x_ref, cot_ref, gain_ref, sel_ref, up_hbm, down_hbm, routes_ref,
    mixed_ref, dtok_ref, dup_hbm, ddown_hbm, dsel_ref,
    up_ref, down_ref, dup_ref, ddown_ref, own_sem,
    ax, ac, a1, a2, asel,
    pbuf, nbuf, qbuf, rbuf, full, ebuf,
    sb, sib, tb, rb, ub, zb,
    pg, ps, pre_k, slope_k, hid_k, dh_k, rows, grads, up_acc, down_acc,
    fn_send, fn_recv, fs_send, fs_recv, fx_send, fx_recv,
    ag_send, ag_recv, az_send, az_recv, as_send, as_recv,
    rs_send, rs_recv, rz_send, rz_recv, rb_send, rb_recv,
):
    Q, F, R, W, H, D = s.chips, s.fsdp, s.rows, s.width, s.hidden, s.model
    T = s.tokens
    HL = H // F
    half = Q * 2 * PAD
    e, z = lax.axis_index("expert"), lax.axis_index("fsdp")
    q, zh, c = e // 4, (e // 2) % 2, e % 2

    def place(q_, zh_, c_):
        return (q_ * 4 + zh_ * 2 + c_, z)

    RC = R // CHUNKS
    par, m = z % 2, z // 2
    near = (e, z + 1 - 2 * par)

    def quad(i):
        return lax.rem(m + i, F // 2)

    far, twin = place(q, 1 - zh, c), place(q, zh, 1 - c)

    def chip(i):
        return lax.rem(q + i, Q)

    def line(i):
        return lax.rem(z + i, F)

    def copy(src, dst, send, recv, device):
        return pltpu.make_async_remote_copy(
            src_ref=src, dst_ref=dst, send_sem=send, recv_sem=recv, device_id=device, device_id_type=MESH
        )

    def each(count, fn):
        lax.fori_loop(1, count, lambda i, t: (fn(i), t)[1], 0)

    def arrived(ref, sem):
        pltpu.make_async_copy(ref, ref, sem).wait()

    pending = []

    def settle():
        for drain in pending:
            drain()
        pending.clear()

    up_in = pltpu.make_async_copy(up_hbm, up_ref, own_sem.at[0])
    down_in = pltpu.make_async_copy(down_hbm, down_ref, own_sem.at[1])
    dup_out = pltpu.make_async_copy(dup_ref, dup_hbm, own_sem.at[2])
    ddown_out = pltpu.make_async_copy(ddown_ref, ddown_hbm, own_sem.at[3])
    up_in.start()
    down_in.start()
    barrier = pltpu.get_barrier_semaphore()

    def greet(device):
        pl.semaphore_signal(barrier, inc=1, device_id=device, device_id_type=MESH)

    each(F, lambda i: greet((e, line(i))))
    each(Q, lambda i: greet(place(chip(i), zh, c)))
    greet(far)
    greet(twin)
    pl.semaphore_wait(barrier, F + Q)

    def ag_hop(k, a, wave, i):
        src = a.at[c, q, zh if wave == 0 else 1 - zh]
        return copy(src, src, ag_send.at[k, wave], ag_recv.at[k, wave], place(chip(i), zh, c))

    def ag_far(k, a):
        src = a.at[c, q, zh]
        return copy(src, src, az_send.at[k], az_recv.at[k], far)

    def ag_twin(k, a):
        return copy(a.at[c], a.at[c], as_send.at[k], as_recv.at[k], twin)

    def ag_start(k, a):
        ag_far(k, a).start()
        each(Q, lambda i: ag_hop(k, a, 0, i).start())

    def ag_forward(k, a):
        ag_far(k, a).wait_recv()
        each(Q, lambda i: ag_hop(k, a, 1, i).start())

    def ag_join(k, a):
        arrived(a.at[c, pl.ds(0, Q - 1), 0], ag_recv.at[k, 0])
        arrived(a.at[c, pl.ds(0, Q - 1), 1], ag_recv.at[k, 1])
        ag_twin(k, a).start()

    def ag_finish(k, a):
        ag_twin(k, a).wait_recv()

        def drain():
            ag_far(k, a).wait_send()
            arrived(a.at[c, pl.ds(0, Q - 1), 0], ag_send.at[k, 0])
            arrived(a.at[c, pl.ds(0, Q - 1), 1], ag_send.at[k, 1])
            ag_twin(k, a).wait_send()

        pending.append(drain)

    def ag_pair_hop(k, a, i):
        src = a.at[c, q]
        return copy(src, src, ag_send.at[k, 0], ag_recv.at[k, 0], place(chip(i), zh, c))

    def ag_pair(k, a):
        each(Q, lambda i: ag_pair_hop(k, a, i).start())

    def ag_pair_join(k, a):
        arrived(a.at[c, pl.ds(0, Q - 1)], ag_recv.at[k, 0])
        ag_twin(k, a).start()

    def ag_pair_finish(k, a):
        ag_twin(k, a).wait_recv()

        def drain():
            arrived(a.at[c, pl.ds(0, Q - 1)], ag_send.at[k, 0])
            ag_twin(k, a).wait_send()

        pending.append(drain)

    def fs_near(k, p):
        src = pbuf.at[k, p, 1 - par]
        return copy(src, nbuf.at[k, p], fn_send.at[k, p], fn_recv.at[k, p], near)

    def fs_hop(k, p, i):
        src, dst = qbuf.at[k, p, quad(i)], rbuf.at[k, p, i]
        return copy(src, dst, fs_send.at[k, p], fs_recv.at[k, p], (e, 2 * quad(i) + par))

    def fs_ext(k, i):
        return copy(ebuf.at[k, 0], ebuf.at[k, i], fx_send.at[k], fx_recv.at[k], (e, line(i)))

    def fs_fill(k, part_of):
        for p in range(CHUNKS):
            value = part_of(slice(p * RC, (p + 1) * RC))
            for j in range(F):
                pbuf[k, p, j % 2, j // 2] = value[:, j * HL : (j + 1) * HL].astype(BF)
            fs_near(k, p).start()

    def fs_spread(k):
        for p in range(CHUNKS):
            fs_near(k, p).wait_recv()
            qbuf[k, p] = (pbuf[k, p, par].astype(F32) + nbuf[k, p].astype(F32)).astype(BF)
            each(F // 2, lambda i: fs_hop(k, p, i).start())

        def drain():
            for p in range(CHUNKS):
                fs_near(k, p).wait_send()
                arrived(rbuf.at[k, p, pl.ds(1, F // 2 - 1)], fs_send.at[k, p])

        pending.append(drain)

    def fs_sum(k, p):
        arrived(rbuf.at[k, p, pl.ds(1, F // 2 - 1)], fs_recv.at[k, p])
        total = qbuf[k, p, m].astype(F32)
        for i in range(1, F // 2):
            total = total + rbuf[k, p, i].astype(F32)
        return total

    def ext_start(k, value):
        ebuf[k, 0] = value
        each(F, lambda i: fs_ext(k, i).start())
        pending.append(lambda: arrived(ebuf.at[k, pl.ds(1, F - 1)], fx_send.at[k]))

    def ext_sum(k):
        arrived(ebuf.at[k, pl.ds(1, F - 1)], fx_recv.at[k])
        total = ebuf[k, 0]
        for i in range(1, F):
            total = total + ebuf[k, i]
        return total

    def fg_hop(k, p, i):
        src = full.at[k, p, par, m]
        return copy(src, src, fs_send.at[4 + k, p], fs_recv.at[4 + k, p], (e, 2 * quad(i) + par))

    def fg_near(k, p):
        src = full.at[k, p, par]
        return copy(src, src, fn_send.at[4 + k, p], fn_recv.at[4 + k, p], near)

    def fg_start(k, p, value):
        full[k, p, par, m] = value
        each(F // 2, lambda i: fg_hop(k, p, i).start())

    def fg_forward(k):
        for p in range(CHUNKS):
            arrived(full.at[k, p, par, pl.ds(0, F // 2 - 1)], fs_recv.at[4 + k, p])
            fg_near(k, p).start()

    def fg_wait(k):
        for p in range(CHUNKS):
            fg_near(k, p).wait_recv()

        def drain():
            for p in range(CHUNKS):
                fg_near(k, p).wait_send()
                arrived(full.at[k, p, par, pl.ds(0, F // 2 - 1)], fs_send.at[4 + k, p])

        pending.append(drain)

    def fg_value(k):
        parts = [
            jnp.concatenate([full[k, p, j % 2, j // 2] for j in range(F)], axis=1) for p in range(CHUNKS)
        ]
        return jnp.concatenate(parts, axis=0)

    def rs_twin(k):
        return copy(sb.at[k], sib.at[k], rb_send.at[k], rb_recv.at[k], twin)

    def rs_hop(k, i):
        return copy(tb.at[k, chip(i)], rb.at[k, i], rs_send.at[k], rs_recv.at[k], place(chip(i), zh, c))

    def rs_far(k):
        if k % 2:
            return copy(ub.at[k, 1 - zh], zb.at[k, 1 - zh], rz_send.at[k], rz_recv.at[k], far)
        return copy(ub.at[k], zb.at[k], rz_send.at[k], rz_recv.at[k], far)

    def rs_start(k, loop, value):
        theirs = dot(ps[loop, 1 - c], value, 1, 0)
        sb[k] = theirs.astype(BF).reshape(Q, 2, PAD, W)
        rs_twin(k).start()
        tb[k] = dot(ps[loop, c], value, 1, 0).astype(BF).reshape(Q, 2, PAD, W)

    def rs_spread(k):
        rs_twin(k).wait_recv()
        tb[k] = (tb[k].astype(F32) + sib[k].astype(F32)).astype(BF)
        each(Q, lambda i: rs_hop(k, i).start())

    def rs_gather(k):
        arrived(rb.at[k, pl.ds(1, Q - 1)], rs_recv.at[k])
        total = tb[k, q].astype(F32)
        for i in range(1, Q):
            total = total + rb[k, i].astype(F32)
        ub[k] = total.astype(BF)
        rs_far(k).start()

    def rs_total(k):
        rs_far(k).wait_recv()

        def drain():
            rs_twin(k).wait_send()
            arrived(rb.at[k, pl.ds(1, Q - 1)], rs_send.at[k])
            rs_far(k).wait_send()

        pending.append(drain)
        if k % 2:
            return (ub[k, zh].astype(F32) + zb[k, zh].astype(F32))[0:T]
        return ub[k].astype(F32) + zb[k].astype(F32)

    lanes = iota((T, 2 * MARKS), 1)
    named = jnp.zeros((T, 2 * MARKS), jnp.bool_)
    unit = jnp.where(iota((T, T), 0) == iota((T, T), 1), 1.0, 0.0).astype(BF)
    r0, r1 = (dot(unit, routes_ref[i].astype(F32).astype(BF), 1, 1).astype(jnp.int32) for i in range(2))
    for k in range(s.top):
        chosen = jnp.where(lanes < MARKS, r0[:, k : k + 1], r1[:, k : k + 1] + MARKS)
        named = named | (chosen == lanes)
    marks = jnp.where(named, 1.0, 0.0)
    earlier = jnp.zeros((T, 2 * MARKS), F32)
    t_of = iota((T, 2 * MARKS), 0)
    for t in range(T - 1):
        earlier = earlier + jnp.where(t_of > t, marks[t : t + 1], 0.0)
    ax[c, q, zh] = jnp.zeros((PAD, W + 2 * MARKS), BF)
    ax[c, q, zh, 0:T, 0:W] = x_ref[...]
    ax[c, q, zh, 0:T, W:] = (marks * (1.0 + earlier)).astype(BF)
    ag_start(0, ax)
    ac[c, q, zh] = jnp.zeros((PAD, W), BF)
    ac[c, q, zh, 0:T] = cot_ref[...]
    gain = gain_ref[...]
    sel_pick = jnp.where(iota((8, s.experts), 1) == e, 1.0, 0.0).astype(BF)
    sel_row = dot(sel_pick, sel_ref[...], 1, 0)

    ag_forward(0, ax)
    ag_join(0, ax)
    ag_finish(0, ax)

    n = 2 * half

    def marks_table():
        return ax[:, :, :, :, W:].reshape(n, 2 * MARKS)

    def build_gather(loop):
        table = marks_table()
        mine = iota((8, 2 * MARKS), 1) == e + loop * MARKS
        wide = dot(jnp.where(mine, 1.0, 0.0).astype(BF), table, 1, 1)[0:1]
        wide_i = wide.astype(jnp.int32)
        row = jnp.where(wide_i > 0, 3 * (iota((1, n), 1) // PAD) + wide_i - 1, -1)
        pg[loop] = jnp.where(iota((R, n), 0) == row, 1.0, 0.0).astype(BF)

    def build_scatter(loop):
        table = marks_table()
        picked = iota((n, 2 * MARKS), 1) == e + loop * MARKS
        tall = jnp.sum(jnp.where(picked, table.astype(F32), 0.0), axis=1, keepdims=True).astype(jnp.int32)
        place_ = jnp.where(tall > 0, 3 * (iota((n, 1), 0) // PAD) + tall - 1, -1)
        ps[loop] = (
            jnp.where(iota((n, R), 1) == place_, 1.0, 0.0).astype(BF).reshape(2, half, R)
        )

    def gathered(a):
        return a[:, :, :, :, 0:W].reshape(2 * half, W)

    def forward_in(loop, a):
        xr = dot(pg[loop], gathered(a), 1, 0)
        rows[loop] = xr.astype(BF)
        y = xr * gain
        yb = y.astype(BF)
        fs_fill(loop, lambda part: dot(yb[part], up_ref[...], 1, 0))
        squares = dot(jnp.ones((8, W), BF), (xr * xr).astype(BF), 1, 1)
        logits = dot(sel_row.astype(BF), yb, 1, 1)
        ext_start(loop, two_rows(squares, logits))

    def forward_mid(loop):
        ext = ext_sum(loop)
        inv_l = lax.rsqrt(ext[0:1] / D + EPSILON)
        logit_l = ext[1:2] * inv_l
        gate_l = jax.nn.sigmoid(logit_l)
        inv, gate = column(inv_l), column(gate_l)
        st = SimpleNamespace(inv=inv, gate=gate, gate_l=gate_l, logit_l=logit_l)
        for p in range(CHUNKS):
            part = slice(p * RC, (p + 1) * RC)
            pre = fs_sum(loop, p) * inv[part]
            sig = jax.nn.sigmoid(pre)
            hid = (pre * sig).astype(BF)
            slope = sig * (1.0 + pre * (1.0 - sig))
            pre_k[loop, part] = pre
            slope_k[loop, part] = slope
            hid_k[loop, part] = hid
            if loop == 0:
                fg_start(0, p, hid)
            else:
                fg_start(3, p, (gate[part] * dh_k[1, part] * slope).astype(BF))
        return st

    def forward_out(loop, st, k):
        out = dot(fg_value(loop), down_ref[...], 1, 0).astype(BF).astype(F32)
        rs_start(k, loop, (st.gate * out).astype(BF))

    def backward_in(loop, a):
        gr = dot(pg[loop], gathered(a), 1, 0).astype(BF)
        grads[loop] = gr
        fs_fill(2 + loop, lambda part: dot(gr[part], down_ref[...], 1, 1))

    def backward_mid(loop, st):
        for p in range(CHUNKS):
            part = slice(p * RC, (p + 1) * RC)
            dh = fs_sum(2 + loop, p)
            dh_k[loop, part] = dh
            fg_start(2 + loop, p, (st.gate[part] * dh * slope_k[loop, part]).astype(BF))

    def backward_ext(loop, st):
        dh = dh_k[loop]
        hg = (st.gate * dh * slope_k[loop]).astype(BF)
        ones = jnp.ones((8, HL), BF)
        gg = dot(ones, (hid_k[loop].astype(F32) * dh).astype(BF), 1, 1)
        inner = dot(ones, (hg.astype(F32) * pre_k[loop]).astype(BF), 1, 1)
        ext_start(2 + loop, two_rows(gg, inner))

    def backward_out(loop, st, k):
        ext = ext_sum(2 + loop)
        lgr_l = ext[0:1] * st.gate_l * (1.0 - st.gate_l)
        inner_l = ext[1:2] + lgr_l * st.logit_l
        lgr, inner = column(lgr_l), column(inner_l)
        fg_wait(2 + loop)
        bg = dot(fg_value(2 + loop), up_ref[...], 1, 1).astype(BF).astype(F32)
        xr = rows[loop].astype(F32)
        ng = bg + lgr * sel_row[0:1]
        contribution = st.inv * gain * ng - (st.inv * st.inv / D) * inner * xr
        rs_start(k, loop, contribution.astype(BF))
        return lgr_l

    def normed(loop, st):
        return (rows[loop].astype(F32) * st.inv * gain).astype(BF)

    def d_sent(loop, st):
        return (grads[loop].astype(F32) * st.gate).astype(BF)

    build_gather(0)
    up_in.wait()
    forward_in(0, ax)
    ag_start(1, ac)
    build_scatter(0)
    build_gather(1)
    fs_spread(0)
    build_scatter(1)
    ag_forward(1, ac)
    st0 = forward_mid(0)
    ag_join(1, ac)
    fg_forward(0)
    ag_finish(1, ac)
    fg_wait(0)
    down_in.wait()
    forward_out(0, st0, 0)
    rs_spread(0)
    backward_in(1, ac)
    rs_gather(0)
    fs_spread(3)
    both = ax[c, q, :, :, 0:W].astype(F32)
    a1[c, q] = (both + rs_total(0)).astype(BF)
    ag_pair(2, a1)
    for p in range(CHUNKS):
        dh_k[1, p * RC : (p + 1) * RC] = fs_sum(3, p)
    ag_pair_join(2, a1)
    ag_pair_finish(2, a1)
    forward_in(1, a1)
    settle()
    fs_spread(1)
    st1 = forward_mid(1)
    backward_ext(1, st1)
    fg_forward(3)
    lgr1_l = backward_out(1, st1, 2)
    for p in range(CHUNKS):
        fg_start(1, p, hid_k[1, p * RC : (p + 1) * RC])
    rs_spread(2)
    n1 = normed(1, st1)
    up_acc[...] = dot(n1, fg_value(3), 0, 0)
    fg_forward(1)
    rs_gather(2)
    sel_acc = dot(jnp.broadcast_to(lgr1_l, (8, R)).astype(BF), n1, 1, 0)
    fg_wait(1)
    down_acc[...] = dot(fg_value(1), d_sent(1, st1), 0, 0)
    both = ac[c, q].astype(F32)
    a2[c, q] = (both + rs_total(2)).astype(BF)
    ag_pair(3, a2)
    forward_out(1, st1, 1)
    ag_pair_join(3, a2)
    ag_pair_finish(3, a2)
    backward_in(0, a2)
    settle()
    rs_spread(1)
    fs_spread(2)
    ddown_ref[...] = (down_acc[...] + dot(fg_value(0), d_sent(0, st0), 0, 0)).astype(BF)
    ddown_out.start()
    n0 = normed(0, st0)
    backward_mid(0, st0)
    backward_ext(0, st0)
    rs_gather(1)
    fg_forward(2)
    lgr0_l = backward_out(0, st0, 3)
    rs_spread(3)
    sel_acc = sel_acc + dot(jnp.broadcast_to(lgr0_l, (8, R)).astype(BF), n0, 1, 0)
    tile = jnp.zeros((8, 128), F32)
    for i in range(W // 128):
        tile = jnp.where(iota((8, 128), 0) == i, sel_acc[:, i * 128 : (i + 1) * 128], tile)
    asel[c, q, zh] = tile
    ag_start(4, asel)
    settle()
    up0 = dot(n0, fg_value(2), 0, 0)
    dup_ref[...] = (up_acc[...] + up0).astype(BF)
    dup_out.start()
    mixed_ref[...] = (a1[c, q, zh, 0:T].astype(F32) + rs_total(1)).astype(BF)
    ag_forward(4, asel)
    rs_gather(3)
    ag_join(4, asel)
    ag_finish(4, asel)
    for i in range(W // 128):
        stack = asel[:, :, :, i, :].reshape(2, 2 * Q, 128)
        dsel_ref[:, i * 128 : (i + 1) * 128] = jnp.stack([stack[0], stack[1]], axis=1).reshape(4 * Q, 128)
    dtok_ref[...] = (a2[c, q, zh, 0:T].astype(F32) + rs_total(3)).astype(BF)
    dup_out.wait()
    ddown_out.wait()
    settle()


def shards(s, tokens, gain, w_sel, w_up, w_down, routes, cotangent):
    Q, F, R, W, H = s.chips, s.fsdp, s.rows, s.width, s.hidden
    HL, NC = H // F, CHUNKS
    RC = R // NC
    VM, DMA = pltpu.VMEM, pltpu.SemaphoreType.DMA
    half = Q * 2 * PAD
    gather = lambda w, t=BF, r=PAD: VM((2, Q, 2, r, w), t)
    scratch = [
        VM((W, H), BF), VM((H, W), BF), VM((W, H), BF), VM((H, W), BF), DMA((4,)),
        gather(W + 2 * MARKS), gather(W), gather(W), gather(W), gather(128, F32, 8),
        VM((4, NC, 2, F // 2, RC, HL), BF), VM((4, NC, F // 2, RC, HL), BF), VM((4, NC, F // 2, RC, HL), BF),
        VM((4, NC, F // 2, RC, HL), BF), VM((4, NC, 2, F // 2, RC, HL), BF), VM((4, F, 8, R), F32),
        VM((4, Q, 2, PAD, W), BF), VM((4, Q, 2, PAD, W), BF), VM((4, Q, 2, PAD, W), BF), VM((4, Q, 2, PAD, W), BF),
        VM((4, 2, PAD, W), BF), VM((4, 2, PAD, W), BF),
        VM((2, R, 2 * half), BF), VM((2, 2, half, R), BF),
        VM((2, R, HL), F32), VM((2, R, HL), F32), VM((2, R, HL), BF), VM((2, R, HL), F32),
        VM((2, R, W), BF), VM((2, R, W), BF), VM((W, H), F32), VM((H, W), F32),
        DMA((8, NC)), DMA((8, NC)), DMA((8, NC)), DMA((8, NC)), DMA((4,)), DMA((4,)),
        DMA((5, 2)), DMA((5, 2)), DMA((5,)), DMA((5,)), DMA((5,)), DMA((5,)),
        DMA((4,)), DMA((4,)), DMA((4,)), DMA((4,)), DMA((4,)), DMA((4,)),
    ]
    T = tokens.shape[0]
    vmem, hbm = pl.BlockSpec(memory_space=pltpu.VMEM), pl.BlockSpec(memory_space=pl.ANY)
    out = pl.pallas_call(
        functools.partial(kernel, s),
        out_shape=(
            jax.ShapeDtypeStruct((T, W), BF),
            jax.ShapeDtypeStruct((T, W), BF),
            jax.ShapeDtypeStruct((W, H), BF),
            jax.ShapeDtypeStruct((H, W), BF),
            jax.ShapeDtypeStruct((s.experts, W), F32),
        ),
        in_specs=[vmem] * 4 + [hbm] * 2 + [vmem],
        out_specs=[vmem] * 2 + [hbm] * 2 + [vmem],
        scratch_shapes=scratch,
        compiler_params=pltpu.CompilerParams(
            collective_id=0, has_side_effects=True, vmem_limit_bytes=60 * 1024 * 1024
        ),
        cost_estimate=pl.CostEstimate(flops=6 * 10**9, bytes_accessed=5 * 2**20, transcendentals=10**5),
    )(tokens, cotangent, gain.reshape(1, W), w_sel.T, w_up[0], w_down[0], routes.swapaxes(1, 2))
    mixed, d_tokens, d_up, d_down, d_sel = out
    return mixed, d_tokens, d_up[None], d_down[None], d_sel.T


def solution(mesh):
    n_expert, fsdp = mesh.shape["expert"], mesh.shape["fsdp"]

    def whole(tokens, gain, w_sel, w_up, w_down, routes, cotangent):
        s = SimpleNamespace(
            chips=n_expert // 4,
            fsdp=fsdp,
            tokens=tokens.shape[0] // n_expert,
            rows=n_expert * 3,
            width=tokens.shape[1] // fsdp,
            model=tokens.shape[1],
            hidden=w_up.shape[2],
            experts=w_sel.shape[1],
            top=routes.shape[2],
        )
        return jax.shard_map(
            functools.partial(shards, s),
            mesh=mesh,
            in_specs=(
                P("expert", "fsdp"),
                P("fsdp"),
                P("fsdp", None),
                P("expert", "fsdp", None),
                P("expert", None, "fsdp"),
                P(None, "expert", None),
                P("expert", "fsdp"),
            ),
            out_specs=(
                P("expert", "fsdp"),
                P("expert", "fsdp"),
                P("expert", "fsdp", None),
                P("expert", None, "fsdp"),
                P("fsdp", None),
            ),
            check_vma=False,
        )(tokens, gain, w_sel, w_up, w_down, routes, cotangent)

    return whole
```
